32 devices in a mesh: trav: 4 (over z), bulk: 8 (over y, x, core).
Axes of the slice: x: 2, y: 2, z: 4, core: 2. Of those that a mesh axis runs over, the one named last changes fastest.
Arguments:
- parents: bfloat16 [6144, 1024], P(('trav', 'bulk')), may hold values from -6 to 6
- act_table: bfloat16 [128, 1024], replicated, may hold values from -5 to 5
- bucket_table: bfloat16 [2048, 1024], P('bulk'), may hold values from -5 to 5
- w_first: bfloat16 [1024, 2048], P(('trav', 'bulk')), may hold values from -0.1875 to 0.1875
- b_first: float32 [2048], replicated, may hold values from -3 to 3
- w_second: bfloat16 [2048, 2048], P(('trav', 'bulk')), may hold values from -0.1875 to 0.1875
- b_second: float32 [2048], replicated, may hold values from -3 to 3
- w_head: bfloat16 [2048, 8], replicated, may hold values from -0.1875 to 0.1875
- b_head: float32 [8], replicated, may hold values from -3 to 3
- branch_counts: int32 [6144], P(('trav', 'bulk')), may hold values from 1 to 4
- sampled_actions: int32 [6144, 4], P(('trav', 'bulk')), may hold values from 0 to 127
- bucket_owner: int32 [6144, 1], P(('trav', 'bulk')), may hold values from 0 to 7; in each aligned block of 192 rows (0 to 191, 192 to 383, ...) at most 32 rows name the same one
- bucket_row: int32 [6144], P(('trav', 'bulk')), may hold values from 0 to 255
- legal_mask: int32 [6144, 32], P(('trav', 'bulk')), may hold values 0 or 1
- ancestor: int32 [6144], P(('trav', 'bulk')), may hold values from 0 to 47
Outputs:
- strategy: float32 [6144, 32], P(('trav', 'bulk'))
- ancestor_value: float32 [1536], P(('trav', 'bulk'))
The draws below stay inside these ranges and needn't reach their ends.
Inputs may be any that keep to these rules, and one draw needn't show every extreme that they name: `bucket_owner`: in each aligned block of 192 histories (the histories of one device) no evaluator is named more than 32 times, a bound that some block reaches.
All inputs are finite; a program needn't handle non-finite values. No bound on the sum of `legal_mask` on one device may be relied on, other than what follows from the above.
Results may differ from the reference program's by a relative error of at most 0.0078.
Values may be sent and summed in bfloat16 or wider, within the bound.
No kernel may reach another device: no remote copies, remote signals or barrier semaphores. Data moves between devices by JAX's collectives and lax.ppermute only.
A program may use at most 64 MiB of HBM per device.

```python
import math
import jax
import jax.numpy as jnp
import numpy as np
from jax import lax

F = 1024
H = 2048
ACTIONS = 8
KMAX = 4
ACT_VOCAB = 128
BUCK_DEV = 256
PAR_DEV = 192
NPAR = 6144
CAP = 32
BUCKETS = 2048
ANC_DEV = 48
ANCESTORS = 1536
N_BULK = 8


def touch_ends(array, stream_key, smallest, top_value):
    longest = array.shape.index(max(array.shape))
    spots = []
    for shift in (0, 1):
        where = [jax.random.randint(jax.random.fold_in(stream_key, axis), (), 0, length) for axis, length in enumerate(array.shape)]
        where[longest] = (where[longest] + shift) % array.shape[longest]
        spots.append(tuple(where))
    return array.at[spots[0]].set(smallest).at[spots[1]].set(top_value)


def block_levels(stream_key, shape, shards, smallest, high):
    loudness = 1.0
    for dim, blocks in shards:
        steps = jax.random.uniform(jax.random.fold_in(jax.random.fold_in(stream_key, 6), dim), (blocks,), jnp.float32, smallest / len(shards), high / len(shards))
        loudness = loudness * jnp.repeat(jnp.exp(steps), shape[dim] // blocks).reshape((-1,) + (1,) * (len(shape) - 1 - dim))
    return loudness


def deal_out(stream_key, own, number, rows, number_of, top, limit, slope):
    ranking = jax.random.permutation(stream_key, number_of)
    heavy_load, ordinary = portions_of(number_of, rows * top, limit, slope, True), portions_of(number_of, rows * top, limit, slope, False)
    places = jnp.arange(number_of)

    def named(tallies, rotation):
        used = int((tallies > 0).sum())
        fixed = max(1, used // 4)
        moved = fixed + (places - fixed + rotation * (used - fixed)) % max(1, number_of - fixed)
        return jnp.zeros((number_of,), jnp.int32).at[ranking[jnp.where(places < fixed, places, moved)]].set(jnp.asarray(tallies, jnp.int32))

    tallies = jnp.where(number % 4 == 0, named(heavy_load, number // 4), named(ordinary, number - number // 4 - 1))
    mixed = jax.random.permutation(jax.random.fold_in(own, 3), number_of)
    donor, receiver = mixed[0:number_of // 2 * 2:2], mixed[1:number_of // 2 * 2:2]
    margin = jnp.minimum(tallies[donor] - 1, limit - tallies[receiver]) // 2
    margin = jnp.where((donor == ranking[0]) | (receiver == ranking[0]) | (tallies[receiver] == 0), 0, jnp.maximum(margin, 0))
    moved = jax.random.randint(jax.random.fold_in(own, 4), (number_of // 2,), 0, 1 << 20) % (margin + 1)
    tallies = tallies.at[donor].add(-moved).at[receiver].add(moved)
    labels = jnp.searchsorted(jnp.cumsum(tallies), jnp.arange(rows * top), side="right").astype(jnp.int32)
    table = labels.reshape(top, rows).T
    table = table[jax.random.permutation(jax.random.fold_in(own, 1), rows)]
    rotation = jax.random.randint(jax.random.fold_in(own, 2), (rows, 1), 0, top)
    return jnp.take_along_axis(table, (jnp.arange(top)[None, :] + rotation) % top, axis=1)


def portions_of(number_of, total, most, slope, full):
    weights = [(1 << 20) // math.isqrt(grade ** slope) + 1 for grade in range(1, number_of + 1)]
    largest = most if full else min(most, max(-(-total // number_of), total * weights[0] // sum(weights)))
    least = 1 if total - largest >= number_of - 1 else 0
    given, surplus = [largest] + [least] * (number_of - 1), total - largest - least * (number_of - 1)
    while surplus > 0:
        free = [i for i in range(1, number_of) if given[i] < largest] or [i for i in range(1, number_of) if given[i] < most]
        pool, left = sum([weights[i] for i in free]), surplus
        for i in free:
            more = min(most - given[i], max(1, left * weights[i] // pool), surplus)
            given[i] = given[i] + more
            surplus = surplus - more
    return np.array(given)


def scatter_about(key, shape, scale, most, cuts=(), held_as=jnp.bfloat16):
    drawn = scale * jax.random.normal(key, shape, jnp.float32)
    if cuts:
        drawn = drawn * block_levels(key, shape, cuts, -0.22, 0.18)
    return jnp.clip(drawn, -most, most).astype(held_as)


def setup_inputs(seed: int = 0) -> dict:
    keys = jax.random.split(jax.random.key(seed), 16)
    parents = scatter_about(keys[0], (NPAR, F), 1.0, 6.0, ((0, 32),))
    act_table = scatter_about(keys[1], (ACT_VOCAB, F), 0.7, 5.0)
    bucket_table = scatter_about(keys[2], (BUCKETS, F), 0.7, 5.0, ((0, 8),))
    w_first = scatter_about(keys[3], (F, H), F ** -0.5, 0.1875, ((0, 32),))
    b_first = scatter_about(keys[4], (H,), 0.5, 3.0, (), jnp.float32)
    w_second = scatter_about(keys[5], (H, H), (H // 2) ** -0.5, 0.1875, ((0, 32),))
    b_second = scatter_about(keys[6], (H,), 0.5, 3.0, (), jnp.float32)
    w_head = scatter_about(keys[7], (H, ACTIONS), (H // 2) ** -0.5, 0.1875)
    b_head = scatter_about(keys[8], (ACTIONS,), 0.5, 3.0, (), jnp.float32)
    branch_counts = touch_ends(jax.random.randint(keys[9], (NPAR,), 1, KMAX + 1), jax.random.fold_in(keys[9], 1), 1, KMAX).astype(jnp.int32)
    sampled_actions = touch_ends(jax.random.randint(keys[10], (NPAR, KMAX), 0, ACT_VOCAB), jax.random.fold_in(keys[10], 1), 0, ACT_VOCAB - 1).astype(jnp.int32)
    bucket_owner_keys = jax.random.split(jax.random.fold_in(keys[11], 1), NPAR // PAR_DEV)
    bucket_owner_turns = jax.random.permutation(jax.random.fold_in(keys[11], 3), NPAR // PAR_DEV)
    bucket_owner = jax.vmap(lambda own, number: deal_out(jax.random.fold_in(keys[11], 2), own, number, PAR_DEV, N_BULK, 1, CAP, 2))(bucket_owner_keys, bucket_owner_turns).reshape((NPAR, 1))
    bucket_row = touch_ends(jax.random.randint(keys[12], (NPAR,), 0, BUCK_DEV), jax.random.fold_in(keys[12], 1), 0, BUCK_DEV - 1).astype(jnp.int32)
    legal_mask = touch_ends((jax.random.randint(keys[13], (NPAR, KMAX * ACTIONS), 0, 2) < 1).astype(jnp.int32), jax.random.fold_in(keys[13], 1), 0, 1)
    ancestor = touch_ends(jax.random.randint(keys[14], (NPAR,), 0, ANC_DEV), jax.random.fold_in(keys[14], 1), 0, ANC_DEV - 1).astype(jnp.int32)
    return {"parents": parents, "act_table": act_table, "bucket_table": bucket_table, "w_first": w_first, "b_first": b_first, "w_second": w_second, "b_second": b_second, "w_head": w_head, "b_head": b_head, "branch_counts": branch_counts, "sampled_actions": sampled_actions, "bucket_owner": bucket_owner, "bucket_row": bucket_row, "legal_mask": legal_mask, "ancestor": ancestor}


tremble = 0.05


def network(inputs, w_first, b_first, w_second, b_second, w_head, b_head):
    first = jnp.dot(inputs, w_first, preferred_element_type=jnp.float32) + b_first
    hidden_one = jnp.maximum(first, 0.0).astype(jnp.bfloat16)
    second = jnp.dot(hidden_one, w_second, preferred_element_type=jnp.float32) + b_second
    hidden_two = jnp.maximum(second, 0.0).astype(jnp.bfloat16)
    return jnp.dot(hidden_two, w_head, preferred_element_type=jnp.float32) + b_head


def reference(parents, act_table, bucket_table, w_first, b_first, w_second, b_second, w_head, b_head, branch_counts, sampled_actions, bucket_owner, bucket_row, legal_mask, ancestor):
    blocks = NPAR // PAR_DEV
    buckets_all = (bucket_owner[:, 0] * BUCK_DEV + bucket_row).astype(jnp.int32)
    first_action = (jnp.arange(ACTIONS) == 0).astype(jnp.float32)

    def one_block(index):
        begin = (index * PAR_DEV).astype(jnp.int32)
        par_rows = lax.dynamic_slice_in_dim(parents, begin, PAR_DEV, 0)
        actions = lax.dynamic_slice_in_dim(sampled_actions, begin, PAR_DEV, 0)
        buckets = lax.dynamic_slice_in_dim(buckets_all, begin, PAR_DEV, 0)
        counts = lax.dynamic_slice_in_dim(branch_counts, begin, PAR_DEV, 0)
        legal = lax.dynamic_slice_in_dim(legal_mask, begin, PAR_DEV, 0)
        act_rows = jnp.take(act_table, actions.reshape(-1), axis=0).reshape(PAR_DEV, KMAX, F)
        base = (par_rows.astype(jnp.float32)[:, None, :] + act_rows.astype(jnp.float32)).astype(jnp.bfloat16)
        base = lax.optimization_barrier(base)
        bucket_rows = jnp.take(bucket_table, buckets, axis=0)
        inputs = (base.astype(jnp.float32) + bucket_rows.astype(jnp.float32)[:, None, :]).astype(jnp.bfloat16)
        advantage = network(inputs.reshape(PAR_DEV * KMAX, F), w_first, b_first, w_second, b_second, w_head, b_head)
        advantage = advantage.reshape(PAR_DEV, KMAX, ACTIONS)
        allowed = jnp.maximum(legal.reshape(PAR_DEV, KMAX, ACTIONS).astype(jnp.float32), first_action)
        positive = allowed * (jnp.maximum(advantage, 0.0) + tremble)
        sigma = positive / jnp.sum(positive, axis=-1, keepdims=True)
        live = (jnp.arange(KMAX)[None, :] < counts[:, None]).astype(jnp.float32)
        strategy = sigma * live[:, :, None]
        branch_value = jnp.sum(sigma * advantage, axis=-1)
        history_value = jnp.sum(branch_value * live, axis=1) / counts.astype(jnp.float32)
        return strategy.reshape(PAR_DEV, KMAX * ACTIONS), history_value

    strategy, history_value = lax.map(one_block, jnp.arange(blocks, dtype=jnp.int32))
    strategy = strategy.reshape(NPAR, KMAX * ACTIONS)
    owner_block = (jnp.arange(NPAR, dtype=jnp.int32) // PAR_DEV).astype(jnp.int32)
    target = (owner_block * ANC_DEV + ancestor).astype(jnp.int32)
    ancestor_value = jax.ops.segment_sum(history_value.reshape(-1), target, num_segments=ANCESTORS)
    return strategy, ancestor_value
```

```python
import functools

import jax
import jax.numpy as jnp
from jax import lax
from jax.experimental import pallas as pl
from jax.experimental.pallas import tpu as pltpu
from jax.sharding import PartitionSpec as P

TREMBLE = 0.05
AXES = ("trav", "bulk")

X, Y, D, A, B, C = 1, 2, 3, 4, 12, 8
ROUNDS = (
    ((X, X, 0), (Y, Y, 0), (A, A, 0), (B, B, 0), (D, D, 0)),
    ((X ^ A, X, A), (Y ^ A, Y, A), (C, A, B), (X ^ B, X, B), (Y ^ B, Y, B), (D ^ B, B, D)),
    ((D ^ A, A, D), (X ^ C, X, C), (Y ^ C, Y, C), (D ^ C, A, D ^ B)),
)


def swap(value, mask):
    count = lax.axis_size("trav") * lax.axis_size("bulk")
    return lax.ppermute(value, AXES, [(i, i ^ mask) for i in range(count)])


def vmem():
    return pl.BlockSpec(memory_space=pltpu.VMEM)


def smem():
    return pl.BlockSpec(memory_space=pltpu.SMEM)


def anywhere():
    return pl.BlockSpec(memory_space=pl.ANY)


def iota(shape, dim):
    return lax.broadcasted_iota(jnp.int32, shape, dim)


def over_rows(a, b):
    return lax.dot_general(a, b, (((0,), (0,)), ((), ())), preferred_element_type=jnp.float32)


OWNER, ROW, COUNT, ANCESTOR, ACTION = 0, 1, 2, 3, 4


def slots_kernel(place, packed, slot, wanted):
    rows = packed.shape[0]
    owners, capacity = wanted.shape
    owner = packed[:, OWNER : OWNER + 1] ^ place[0]
    hits = (owner == iota((rows, owners), 1)).astype(jnp.float32)
    before = (iota((rows, rows), 1) < iota((rows, rows), 0)).astype(jnp.bfloat16)
    earlier = jnp.dot(before, hits.astype(jnp.bfloat16), preferred_element_type=jnp.float32)
    rank = jnp.sum(earlier * hits, axis=1, keepdims=True).astype(jnp.int32)
    slot[...] = owner * capacity + rank
    bucket = (hits * packed[:, ROW : ROW + 1].astype(jnp.float32)).astype(jnp.bfloat16)
    at_rank = (rank == iota((rows, capacity), 1)).astype(jnp.bfloat16)
    wanted[...] = over_rows(bucket, at_rank).astype(jnp.int32)


def rows_kernel(wants, table, *outs):
    buckets = table.shape[0]
    for want, out in zip(wants, outs):
        onehot = (iota((buckets, want.shape[1]), 0) == want).astype(jnp.bfloat16)
        out[...] = over_rows(onehot, table[...]).astype(jnp.bfloat16)


def first_kernel(capacity, sources, pieces_at, place, packed, slot, parents, act_table, bias, *rest):
    n_rows, n_pieces = len(sources), len(pieces_at)
    row_refs, pieces = rest[:n_rows], rest[n_rows : n_rows + n_pieces]
    out, weights, inputs, sems = rest[n_rows + n_pieces :]
    copies = start_pieces(place, pieces, pieces_at, weights, sems)
    rows = parents.shape[0]
    bucket = jnp.zeros(parents.shape, jnp.float32)
    for j, (ref, begin) in enumerate(zip(row_refs, sources)):
        count = capacity if begin is not None else ref.shape[0]
        begin = begin or 0
        onehot = (slot[...] == iota((rows, count), 1) + j * capacity).astype(jnp.bfloat16)
        bucket = bucket + jnp.dot(onehot, ref[begin : begin + count], preferred_element_type=jnp.float32)
    for c in range(inputs.shape[0] // rows):
        onehot = (packed[:, ACTION + c : ACTION + c + 1] == iota((rows, act_table.shape[0]), 1)).astype(jnp.bfloat16)
        change = jnp.dot(onehot, act_table[...], preferred_element_type=jnp.float32)
        base = (parents[...].astype(jnp.float32) + change).astype(jnp.bfloat16)
        inputs[c * rows : (c + 1) * rows, :] = (base.astype(jnp.float32) + bucket).astype(jnp.bfloat16)
    for copy in copies:
        copy.wait()
    step = 512
    for n in range(0, weights.shape[1], step):
        total = jnp.dot(inputs[...], weights[:, n : n + step], preferred_element_type=jnp.float32)
        out[:, n : n + step] = jnp.maximum(total + bias[:, n : n + step], 0.0).astype(jnp.bfloat16)


def start_pieces(place, pieces, pieces_at, weights, sems):
    copies = []
    for j, (piece, (begin, count)) in enumerate(zip(pieces, pieces_at)):
        to = pl.multiple_of((place[1] ^ j) * count, count)
        copies.append(
            pltpu.make_async_copy(piece.at[pl.ds(begin, count)], weights.at[pl.ds(to, count)], sems.at[j])
        )
    for copy in copies:
        copy.start()
    return copies


def second_kernel(pieces_at, place, packed, hidden, bias, w_head, b_head, legal, *rest):
    n_pieces = len(pieces_at)
    pieces = rest[:n_pieces]
    strategy, values, weights, sems = rest[n_pieces:]
    copies = start_pieces(place, pieces, pieces_at, weights, sems)
    for copy in copies:
        copy.wait()
    actions = w_head.shape[1]
    rows = packed.shape[0]
    advantage = jnp.zeros((hidden.shape[0], actions), jnp.float32)
    step = 512
    for n in range(0, weights.shape[1], step):
        total = jnp.dot(hidden[...], weights[:, n : n + step], preferred_element_type=jnp.float32)
        layer = jnp.maximum(total + bias[:, n : n + step], 0.0).astype(jnp.bfloat16)
        advantage = advantage + jnp.dot(layer, w_head[n : n + step, :], preferred_element_type=jnp.float32)
    advantage = advantage + b_head[...]
    counts = packed[:, COUNT : COUNT + 1]
    first_action = (iota((rows, actions), 1) == 0).astype(jnp.float32)
    total_value = jnp.zeros((rows, 1), jnp.float32)
    for c in range(hidden.shape[0] // rows):
        mine = advantage[c * rows : (c + 1) * rows, :]
        allowed = jnp.maximum(legal[:, c * actions : (c + 1) * actions].astype(jnp.float32), first_action)
        positive = allowed * (jnp.maximum(mine, 0.0) + TREMBLE)
        sigma = positive / jnp.sum(positive, axis=1, keepdims=True)
        live = (counts > c).astype(jnp.float32)
        strategy[:, c * actions : (c + 1) * actions] = sigma * live
        total_value = total_value + live * jnp.sum(sigma * mine, axis=1, keepdims=True)
    value = total_value / counts.astype(jnp.float32)
    nodes = values.shape[1]
    at_node = (packed[:, ANCESTOR : ANCESTOR + 1] == iota((rows, nodes), 1)).astype(jnp.float32)
    values[...] = jnp.sum(at_node * value, axis=0, keepdims=True)


def limit(mebibytes):
    return pltpu.CompilerParams(vmem_limit_bytes=mebibytes << 20)


def body(
    parents,
    act_table,
    bucket_table,
    w_first,
    b_first,
    w_second,
    b_second,
    w_head,
    b_head,
    branch_counts,
    sampled_actions,
    bucket_owner,
    bucket_row,
    legal_mask,
    ancestor,
):
    par_count, feature_count = parents.shape
    branch_slots = sampled_actions.shape[1]
    hidden_units = w_first.shape[1]
    bulk_count, trav_count = lax.axis_size("bulk"), lax.axis_size("trav")
    devices = bulk_count * trav_count
    capacity = max(2, (4 * par_count + 3 * bulk_count - 1) // (3 * bulk_count))
    by_xor = (trav_count, bulk_count) == (4, 8)
    bulk_index = lax.axis_index("bulk")
    index = lax.axis_index("trav") * bulk_count + bulk_index
    zero = jnp.zeros_like(index)
    place = jnp.stack([bulk_index, index] if by_xor else [zero, zero]).astype(jnp.int32)

    packed = jnp.concatenate(
        [bucket_owner, bucket_row[:, None], branch_counts[:, None], ancestor[:, None], sampled_actions], axis=1
    )

    w_both = jnp.concatenate([w_first, w_second], axis=0)
    depth_one, depth_two = w_first.shape[0], w_second.shape[0]

    slot, wanted = pl.pallas_call(
        slots_kernel,
        out_shape=(
            jax.ShapeDtypeStruct((par_count, 1), jnp.int32),
            jax.ShapeDtypeStruct((bulk_count, capacity), jnp.int32),
        ),
        in_specs=[smem(), vmem()],
        out_specs=(vmem(), vmem()),
    )(place, packed)

    if by_xor:
        held = {0: w_both}
        for arriving, partner, piece in ROUNDS[0]:
            held[arriving] = swap(held[piece], partner << 1)

        both = jnp.concatenate([wanted, swap(wanted, 1)], axis=0)
        asked = {0: both}
        for chip in (X, Y, D):
            asked[chip] = swap(both, chip << 1)

        def serve(ids_0, ids_x, ids_y, ids_d, table, *outs):
            wants = []
            for chip, ids in zip((0, X, Y, D), (ids_0, ids_x, ids_y, ids_d)):
                mine = [ids[bulk_count * core + 2 * chip + core : bulk_count * core + 2 * chip + core + 1, :] for core in (0, 1)]
                wants.append(jnp.concatenate(mine, axis=1))
            rows_kernel(wants, table, *outs)

        served = pl.pallas_call(
            serve,
            out_shape=(jax.ShapeDtypeStruct((2 * capacity, feature_count), jnp.bfloat16),) * 4,
            in_specs=[vmem()] * 5,
            out_specs=(vmem(),) * 4,
        )(*(asked[chip] for chip in (0, X, Y, D)), bucket_table)
        row_arrays, sources = [], []
        for chip, rows in zip((0, X, Y, D), served):
            mine = swap(rows, chip << 1) if chip else rows
            row_arrays += [mine, swap(mine, 1)]
            sources += [0, capacity]

        for arrivals in ROUNDS[1:]:
            for arriving, partner, piece in arrivals:
                held[arriving] = swap(held[piece], partner << 1)
        pieces = []
        for chip in range(devices // 2):
            pieces += [held[chip], swap(held[chip], 1)]
        first_at = [(0, depth_one)] * devices
        second_at = [(depth_one, depth_two)] * devices
        first_pieces = second_pieces = pieces
    else:
        asked = lax.all_to_all(wanted, "bulk", split_axis=0, concat_axis=0, tiled=True)
        served = jnp.take(bucket_table, asked.reshape(-1), axis=0)
        served = served.reshape(bulk_count, capacity, feature_count)
        arrived = lax.all_to_all(served, "bulk", split_axis=0, concat_axis=0, tiled=True)
        row_arrays, sources = [arrived.reshape(bulk_count * capacity, feature_count)], [None]
        first_pieces = [lax.all_gather(w_first, AXES, axis=0, tiled=True)]
        second_pieces = [lax.all_gather(w_second, AXES, axis=0, tiled=True)]
        first_at = [(0, first_pieces[0].shape[0])]
        second_at = [(0, second_pieces[0].shape[0])]

    branches = par_count * branch_slots
    hidden = pl.pallas_call(
        functools.partial(first_kernel, capacity, sources, first_at),
        out_shape=jax.ShapeDtypeStruct((branches, hidden_units), jnp.bfloat16),
        in_specs=[smem()] + [vmem()] * (5 + len(row_arrays)) + [anywhere()] * len(first_pieces),
        out_specs=vmem(),
        scratch_shapes=[
            pltpu.VMEM((feature_count, hidden_units), jnp.bfloat16),
            pltpu.VMEM((branches, feature_count), jnp.bfloat16),
            pltpu.SemaphoreType.DMA((len(first_pieces),)),
        ],
        compiler_params=limit(24),
    )(place, packed, slot, parents, act_table, b_first[None, :], *row_arrays, *first_pieces)

    node_count = par_count // 4
    strategy, values = pl.pallas_call(
        functools.partial(second_kernel, second_at),
        out_shape=(
            jax.ShapeDtypeStruct(legal_mask.shape, jnp.float32),
            jax.ShapeDtypeStruct((1, node_count), jnp.float32),
        ),
        in_specs=[smem()] + [vmem()] * 6 + [anywhere()] * len(second_pieces),
        out_specs=(vmem(), vmem()),
        scratch_shapes=[
            pltpu.VMEM((hidden_units, hidden_units), jnp.bfloat16),
            pltpu.SemaphoreType.DMA((len(second_pieces),)),
        ],
        compiler_params=limit(28),
    )(place, packed, hidden, b_second[None, :], w_head, b_head[None, :], legal_mask, *second_pieces)
    return (strategy, values.reshape(-1))


def solution(mesh):
    return jax.shard_map(
        body,
        mesh=mesh,
        in_specs=(
            P(AXES, None),
            P(),
            P("bulk", None),
            P(AXES, None),
            P(),
            P(AXES, None),
            P(),
            P(),
            P(),
            P(AXES),
            P(AXES, None),
            P(AXES, None),
            P(AXES),
            P(AXES, None),
            P(AXES),
        ),
        out_specs=(P(AXES, None), P(AXES)),
        check_vma=False,
    )
```

```python
import functools

import jax
import jax.numpy as jnp
from jax import lax
from jax.experimental import pallas as pl
from jax.experimental.pallas import tpu as pltpu
from jax.sharding import PartitionSpec as P

TREMBLE = 0.05
AXES = ("trav", "bulk")

TRAV, BULK = 4, 8
X, Y, D, A, B, C = 1, 2, 3, 4, 12, 8
PLANE = (0, X, Y, D)
ID_ROWS = 16

def swap_chip(value, chip):
    return lax.ppermute(value, AXES, [(i, i ^ (chip << 1)) for i in range(TRAV * BULK)])


def swap_core(value):
    return lax.ppermute(value, AXES, [(i, i ^ 1) for i in range(TRAV * BULK)])


def iota(shape, dim):
    return lax.broadcasted_iota(jnp.int32, shape, dim)


def over_rows(a, b):
    return lax.dot_general(a, b, (((0,), (0,)), ((), ())), preferred_element_type=jnp.float32)


def my_core():
    return lax.axis_index("bulk") & 1


def my_chip():
    return lax.axis_index("trav") * (BULK // 2) + (lax.axis_index("bulk") >> 1)


def call(kernel, outs, mebibytes, scratch=(), flops=0, bytes_accessed=0, in_specs=None):
    many = isinstance(outs, (list, tuple))
    spec = pl.BlockSpec(memory_space=pltpu.VMEM)

    def run(*args):
        return pl.pallas_call(
            kernel,
            out_shape=tuple(outs) if many else outs,
            in_specs=in_specs or [spec] * len(args),
            out_specs=(spec,) * len(outs) if many else spec,
            scratch_shapes=list(scratch),
            compiler_params=pltpu.CompilerParams(vmem_limit_bytes=mebibytes << 20),
            cost_estimate=pl.CostEstimate(flops=flops, bytes_accessed=bytes_accessed, transcendentals=0),
        )(*args)

    return run


def shape(rows, columns, dtype=jnp.bfloat16):
    return jax.ShapeDtypeStruct((rows, columns), dtype)


def join_kernel(w_first, w_second, other_first, other_second, wanted, other_wanted, out, out_ids):
    core, half = my_core(), out.shape[1]
    here = pl.ds(pl.multiple_of(core * half, half), half)
    begin = 0
    for mine, other in ((w_first, other_first), (w_second, other_second)):
        depth = mine.shape[0]
        for to, rows in ((core, mine), (1 - core, other)):
            place = pl.ds(pl.multiple_of(begin + to * depth, depth), depth)
            for target in (out, out_ids):
                target[place, :] = rows[:, here]
        begin += 2 * depth
    owners, capacity = wanted.shape
    blank = jnp.zeros((owners, half - 2 * capacity), jnp.float32)
    ids = jnp.concatenate([wanted[...].astype(jnp.float32), other_wanted[...].astype(jnp.float32), blank], axis=1)
    ids = jnp.concatenate([ids, jnp.zeros((out_ids.shape[0] - begin - owners, half), jnp.float32)], axis=0)
    out_ids[begin:, :] = ids.astype(jnp.bfloat16)


def across(a, b, precision=None):
    return lax.dot_general(
        a, b, (((1,), (1,)), ((), ())), preferred_element_type=jnp.float32, precision=precision
    )


def slots_kernel(owner, row, slot, wanted):
    rows = owner.shape[1]
    owners, capacity = wanted.shape
    partner = owner[...] ^ lax.axis_index("bulk")
    hits = (partner == iota((owners, rows), 0)).astype(jnp.float32)
    before = (iota((rows, rows), 0) < iota((rows, rows), 1)).astype(jnp.bfloat16)
    earlier = jnp.dot(hits.astype(jnp.bfloat16), before, preferred_element_type=jnp.float32)
    rank = jnp.sum(earlier * hits, axis=0, keepdims=True).astype(jnp.int32)
    slot[...] = partner * capacity + rank
    bucket = (hits * row[...].astype(jnp.float32)).astype(jnp.bfloat16)
    at_rank = (rank == iota((capacity, rows), 0)).astype(jnp.bfloat16)
    wanted[...] = across(bucket, at_rank).astype(jnp.int32)


def serve_kernel(capacity, *refs):
    asked, table, outs = refs[: len(PLANE)], refs[len(PLANE)], refs[len(PLANE) + 1 :]
    buckets = table.shape[0]
    for chip, ids, out in zip(PLANE, asked, outs):
        owners = ids[ids.shape[0] - ID_ROWS :, :].astype(jnp.int32)
        mine = [owners[2 * chip + core : 2 * chip + core + 1, core * capacity : (core + 1) * capacity] for core in (0, 1)]
        want = jnp.concatenate(mine, axis=1)
        onehot = (iota((buckets, want.shape[1]), 0) == want).astype(jnp.bfloat16)
        out[...] = over_rows(onehot, table[...]).astype(jnp.bfloat16)


def stack_kernel(places, *refs):
    refs, out = refs[:-1], refs[-1]
    to = 0
    for ref, (begin, count) in zip(refs, places):
        out[to : to + count, :] = ref[begin : begin + count, :]
        to += count


def stack(*parts):
    arrays, places = [part[0] for part in parts], [part[1:] for part in parts]
    total = sum(count for _, count in places)
    out = shape(total, arrays[0].shape[1], arrays[0].dtype)
    return call(functools.partial(stack_kernel, places), out, 4)(*arrays)


def inputs_kernel(begins, actions, slot, parents, act_table, *refs):
    same, sibling, inputs = refs[: len(PLANE)], refs[len(PLANE)], refs[len(PLANE) + 1]
    rows = parents.shape[0]
    capacity = sibling.shape[0] // len(PLANE)
    parts = []
    for n, (begin, ref) in enumerate(zip(begins, same)):
        parts += [ref[begin : begin + capacity, :], sibling[n * capacity : (n + 1) * capacity, :]]
    served = jnp.concatenate(parts, axis=0)
    onehot = (slot[...] == iota((served.shape[0], rows), 0)).astype(jnp.bfloat16)
    bucket = over_rows(onehot, served)
    for c in range(actions.shape[0]):
        onehot = (actions[c : c + 1, :] == iota((act_table.shape[0], rows), 0)).astype(jnp.bfloat16)
        change = over_rows(onehot, act_table[...])
        base = (parents[...].astype(jnp.float32) + change).astype(jnp.bfloat16)
        inputs[c * rows : (c + 1) * rows, :] = (base.astype(jnp.float32) + bucket).astype(jnp.bfloat16)


def place_pieces(pieces, refs, depth, weights):
    for chip, which, begin, row, count in pieces:
        to = pl.multiple_of((my_chip() ^ chip) * depth + row, 16)
        weights[pl.ds(to, count), :] = refs[which][begin : begin + count, :]


def line_up(pieces, refs, depth, mine, theirs, weights, picked):
    rows = mine.shape[0] // 2
    chip, core = my_chip(), my_core()
    blocks = mine.shape[1] // depth
    order = list(dict.fromkeys(piece[0] for piece in pieces))
    for name, which, begin, row, count in pieces:
        to = order.index(name) * depth + row
        weights[to : to + count, :] = refs[which][begin : begin + count, :]
    for n, name in enumerate(order):
        there = chip ^ name
        column = pl.ds(pl.multiple_of((there & (blocks - 1)) * depth, depth), depth)
        at_home = (there // blocks) == core
        for m in (0, 1):
            ours = mine[m * rows : (m + 1) * rows, column]
            others = theirs[(1 - m) * rows : (2 - m) * rows, column]
            picked[m * rows : (m + 1) * rows, n * depth : (n + 1) * depth] = jnp.where(at_home, ours, others)


def first_kernel(pieces, depth, mine, theirs, bias, *refs):
    refs, (out, weights) = refs[:-2], refs[-2:]
    place_pieces(pieces, refs, depth, weights)
    rows, half = mine.shape[0], weights.shape[1]
    offset = my_core() * half
    step = 512
    for n in range(0, half, step):
        shift = bias[:, pl.ds(pl.multiple_of(offset + n, step), step)]
        for m, inputs in enumerate((mine, theirs)):
            total = jnp.dot(inputs[...], weights[:, n : n + step], preferred_element_type=jnp.float32)
            out[m * rows : (m + 1) * rows, n : n + step] = jnp.maximum(total + shift, 0.0).astype(jnp.bfloat16)


def second_kernel(pieces, depth, mine, theirs, *refs):
    refs, (out, weights, picked) = refs[:-3], refs[-3:]
    rows, half = mine.shape[0] // 2, weights.shape[1]
    line_up(pieces, refs, depth, mine, theirs, weights, picked)
    step = 512
    for m in (0, 1):
        for n in range(0, half, step):
            out[m * rows : (m + 1) * rows, n : n + step] = jnp.dot(
                picked[m * rows : (m + 1) * rows, :], weights[:, n : n + step], preferred_element_type=jnp.float32
            )


def third_kernel(pieces, depth, mine, theirs, so_far, bias, w_head, *refs):
    refs, (out_mine, out_theirs, weights, picked) = refs[:-4], refs[-4:]
    rows, half = mine.shape[0] // 2, weights.shape[1]
    core = my_core()
    line_up(pieces, refs, depth, mine, theirs, weights, picked)
    step = 512
    for m, out in enumerate((out_mine, out_theirs)):
        advantage = jnp.zeros((rows, w_head.shape[0]), jnp.float32)
        for n in range(0, half, step):
            here = pl.ds(pl.multiple_of(core * half + n, step), step)
            total = so_far[m * rows : (m + 1) * rows, n : n + step] + jnp.dot(
                picked[m * rows : (m + 1) * rows, :], weights[:, n : n + step], preferred_element_type=jnp.float32
            )
            layer = jnp.maximum(total + bias[:, here], 0.0).astype(jnp.bfloat16)
            advantage = advantage + across(layer, w_head[:, here])
        out[...] = advantage.T


def last_kernel(counts, ancestor, legal, b_head, mine, theirs, strategy, values):
    actions = b_head.shape[1]
    rows = counts.shape[1]
    diagonal = iota((actions, actions), 0) == iota((actions, actions), 1)
    shift = jnp.sum(jnp.where(diagonal, b_head[...], 0.0), axis=1, keepdims=True)
    first_action = (iota((actions, rows), 0) == 0).astype(jnp.float32)
    total_value = jnp.zeros((1, rows), jnp.float32)
    for c in range(mine.shape[1] // rows):
        here = slice(c * rows, (c + 1) * rows)
        advantage = mine[:, here] + theirs[:, here] + shift
        allowed = jnp.maximum(legal[c * actions : (c + 1) * actions, :].astype(jnp.float32), first_action)
        positive = allowed * (jnp.maximum(advantage, 0.0) + TREMBLE)
        sigma = positive / jnp.sum(positive, axis=0, keepdims=True)
        live = (counts[...] > c).astype(jnp.float32)
        strategy[c * actions : (c + 1) * actions, :] = sigma * live
        total_value = total_value + live * jnp.sum(sigma * advantage, axis=0, keepdims=True)
    value = total_value / counts[...].astype(jnp.float32)
    at_node = (ancestor[...] == iota((values.shape[1], rows), 0)).astype(jnp.float32)
    values[...] = across(value, at_node, lax.Precision.HIGHEST)


def body(
    parents,
    act_table,
    bucket_table,
    w_first,
    b_first,
    w_second,
    b_second,
    w_head,
    b_head,
    branch_counts,
    sampled_actions,
    bucket_owner,
    bucket_row,
    legal_mask,
    ancestor,
):
    par_count, feature_count = parents.shape
    branches = par_count * sampled_actions.shape[1]
    hidden_units = w_first.shape[1]
    half = hidden_units // 2
    depth_one, depth_two = w_first.shape[0], w_second.shape[0]
    capacity = max(2, (4 * par_count + 3 * BULK - 1) // (3 * BULK))

    slot, wanted = call(
        slots_kernel, (shape(1, par_count, jnp.int32), shape(BULK, capacity, jnp.int32)), 4
    )(bucket_owner.T, bucket_row[None, :])
    depth = 2 * (depth_one + depth_two)
    own, own_ids = call(join_kernel, (shape(depth, half), shape(depth + ID_ROWS, half)), 4)(
        w_first, w_second, swap_core(w_first), swap_core(w_second), wanted, swap_core(wanted)
    )
    from_x, from_y, from_d = [swap_chip(own_ids, chip) for chip in PLANE[1:]]
    from_a, from_b = [swap_chip(own, chip) for chip in (A, B)]
    served = call(
        functools.partial(serve_kernel, capacity), (shape(2 * capacity, feature_count),) * len(PLANE), 6
    )(own_ids, from_x, from_y, from_d, bucket_table)
    ab = ((from_a, 0, depth), (from_b, 0, depth))
    wide = 2 * capacity
    to_x, to_y, to_d = served[1:]
    x_ab = swap_chip(stack(*ab, (to_x, 0, wide)), X)
    y_ab = swap_chip(stack(*ab, (to_y, 0, wide)), Y)
    rows_d = swap_chip(to_d, D)
    from_ab, d_b = swap_chip(from_b, A), swap_chip(stack((from_d, 0, depth)), B)
    x_ab, y_ab, rows_d, from_ab, d_b = lax.optimization_barrier((x_ab, y_ab, rows_d, from_ab, d_b))

    same = [(served[0], 0), (x_ab, 2 * depth), (y_ab, 2 * depth), (rows_d, 0)]
    sibling = swap_core(stack(*((rows, begin + capacity, capacity) for rows, begin in same)))
    inputs = call(
        functools.partial(inputs_kernel, [begin for _, begin in same]), shape(branches, feature_count), 8
    )(sampled_actions.T, slot, parents, act_table, *(rows for rows, _ in same), sibling)
    inputs_sibling = swap_core(inputs)

    chip_one, chip_two = 2 * depth_one, 2 * depth_two

    def later(begin, count, cut):
        x_c = stack((from_ab, begin, count), (y_ab, begin, cut))
        y_c = stack((from_ab, begin, count), *([(x_ab, begin + cut, count - cut)] if cut < count else []))
        return [swap_chip(x_c, X), swap_chip(y_c, Y), swap_chip(stack((d_b, begin, count)), A)]

    def late_pieces(count, cut, first):
        pieces = [(X ^ C, first, 0, 0, count), (Y ^ C, first + 1, 0, 0, count), (D ^ C, first + 2, 0, 0, count)]
        pieces.append((D ^ A, first, count, 0, cut))
        return pieces + ([(D ^ A, first + 1, count, cut, count - cut)] if cut < count else [])

    early_arrays = [own, from_x, from_y, from_a, from_b, from_d, x_ab, y_ab, from_ab, d_b]

    def early_pieces(begin):
        count = chip_two if begin else chip_one
        pieces = [(chip, n, begin) for n, chip in enumerate((0, X, Y, A, B, D))]
        pieces += [(X ^ A, 6, begin), (X ^ B, 6, depth + begin), (Y ^ A, 7, begin), (Y ^ B, 7, depth + begin)]
        pieces += [(C, 8, begin), (D ^ B, 9, begin)]
        return [(*piece, 0, count) for piece in pieces]

    cut_two = chip_two // 4
    first_late, second_late = later(0, chip_one, chip_one), later(chip_one, chip_two, cut_two)
    first_arrays = early_arrays + first_late
    first_pieces = early_pieces(0) + late_pieces(chip_one, chip_one, len(early_arrays))

    hidden = call(
        functools.partial(first_kernel, first_pieces, chip_one),
        shape(2 * branches, half),
        14,
        [pltpu.VMEM((feature_count, half), jnp.bfloat16)],
    )(inputs, inputs_sibling, b_first[None, :], *first_arrays)
    hidden_sibling = swap_core(hidden)

    early, late = early_pieces(chip_one), late_pieces(chip_two, cut_two, 0)
    so_far = call(
        functools.partial(second_kernel, early, chip_two),
        shape(2 * branches, half, jnp.float32),
        16,
        [pltpu.VMEM((len(early) * chip_two, half), jnp.bfloat16), pltpu.VMEM((2 * branches, len(early) * chip_two), jnp.bfloat16)],
    )(hidden, hidden_sibling, *early_arrays)
    mine, theirs = call(
        functools.partial(third_kernel, late, chip_two),
        (shape(w_head.shape[1], branches, jnp.float32),) * 2,
        12,
        [pltpu.VMEM((4 * chip_two, half), jnp.bfloat16), pltpu.VMEM((2 * branches, 4 * chip_two), jnp.bfloat16)],
    )(hidden, hidden_sibling, so_far, b_second[None, :], w_head.T, *second_late)
    strategy, values = call(
        last_kernel, (shape(legal_mask.shape[1], par_count, jnp.float32), shape(1, par_count // 4, jnp.float32)), 4
    )(branch_counts[None, :], ancestor[None, :], legal_mask.T, b_head[None, :], mine, swap_core(theirs))
    return (strategy.T, values.reshape(-1))


def network(inputs, w_first, b_first, w_second, b_second, w_head, b_head):
    columns = inputs
    first = jnp.dot(
        columns,
        lax.all_gather(w_first, ("trav", "bulk"), axis=0, tiled=True),
        preferred_element_type=jnp.float32,
    )
    hidden_one = jnp.maximum(first + b_first, 0.0).astype(jnp.bfloat16)
    columns = hidden_one
    second = jnp.dot(
        columns,
        lax.all_gather(w_second, ("trav", "bulk"), axis=0, tiled=True),
        preferred_element_type=jnp.float32,
    )
    hidden_two = jnp.maximum(second + b_second, 0.0).astype(jnp.bfloat16)
    return jnp.dot(hidden_two, w_head, preferred_element_type=jnp.float32) + b_head


def general_body(
    parents,
    act_table,
    bucket_table,
    w_first,
    b_first,
    w_second,
    b_second,
    w_head,
    b_head,
    branch_counts,
    sampled_actions,
    bucket_owner,
    bucket_row,
    legal_mask,
    ancestor,
):
    par_count = parents.shape[0]
    feature_count = parents.shape[1]
    branch_slots = sampled_actions.shape[1]
    vocab_size = act_table.shape[0]
    action_count = w_head.shape[1]
    bulk_count = lax.axis_size("bulk")
    capacity = max(2, (4 * par_count + 3 * bulk_count - 1) // (3 * bulk_count))
    slot_total = bulk_count * capacity
    action_onehot = (
        sampled_actions.reshape(-1)[:, None] == jnp.arange(vocab_size)[None, :]
    ).astype(jnp.bfloat16)
    act_rows = jnp.dot(action_onehot, act_table, preferred_element_type=jnp.float32)
    base = (jnp.repeat(parents.astype(jnp.float32), branch_slots, axis=0) + act_rows).astype(
        jnp.bfloat16
    )
    base = lax.optimization_barrier(base)
    owner_index = bucket_owner[:, 0]
    owner_hits = (owner_index[:, None] == jnp.arange(bulk_count)[None, :]).astype(jnp.int32)
    earlier = jnp.cumsum(owner_hits, axis=0) - owner_hits
    slot_index = owner_index * capacity + jnp.sum(earlier * owner_hits, axis=1)
    placement_int = (slot_index[None, :] == jnp.arange(slot_total)[:, None]).astype(jnp.int32)
    slot_bucket = jnp.sum(placement_int * bucket_row[None, :], axis=1).reshape(bulk_count, capacity)
    placement = placement_int.astype(jnp.bfloat16)
    outgoing = jnp.dot(
        placement,
        base.reshape(par_count, branch_slots * feature_count),
        preferred_element_type=jnp.float32,
    )
    outgoing = outgoing.astype(jnp.bfloat16).reshape(
        bulk_count, capacity * branch_slots, feature_count
    )
    arrived_rows = lax.all_to_all(outgoing, "bulk", split_axis=0, concat_axis=0, tiled=True)
    arrived_ids = lax.all_to_all(slot_bucket, "bulk", split_axis=0, concat_axis=0, tiled=True)
    table_rows = jnp.take(bucket_table, arrived_ids.reshape(-1), axis=0)
    inputs = (
        arrived_rows.reshape(slot_total, branch_slots, feature_count).astype(jnp.float32)
        + table_rows.astype(jnp.float32)[:, None, :]
    )
    inputs = inputs.astype(jnp.bfloat16).reshape(slot_total * branch_slots, feature_count)
    evaluated = network(inputs, w_first, b_first, w_second, b_second, w_head, b_head)
    returned = lax.all_to_all(
        evaluated.reshape(bulk_count, capacity * branch_slots * action_count).astype(jnp.bfloat16),
        "bulk",
        split_axis=0,
        concat_axis=0,
        tiled=True,
    ).astype(jnp.float32)
    advantage = jnp.take(
        returned.reshape(slot_total, branch_slots * action_count), slot_index, axis=0
    )
    advantage = advantage.reshape(par_count, branch_slots, action_count)
    first_action = (jnp.arange(action_count) == 0).astype(jnp.float32)
    allowed = jnp.maximum(
        legal_mask.reshape(par_count, branch_slots, action_count).astype(jnp.float32), first_action
    )
    positive = allowed * (jnp.maximum(advantage, 0.0) + TREMBLE)
    sigma = positive / jnp.sum(positive, axis=-1, keepdims=True)
    live = (jnp.arange(branch_slots)[None, :] < branch_counts[:, None]).astype(jnp.float32)
    strategy = (sigma * live[:, :, None]).reshape(par_count, branch_slots * action_count)
    branch_value = jnp.sum(sigma * advantage, axis=-1)
    history_value = jnp.sum(branch_value * live, axis=1) / branch_counts.astype(jnp.float32)
    node_count = par_count // 4
    node_onehot = (ancestor[:, None] == jnp.arange(node_count)[None, :]).astype(jnp.float32)
    ancestor_value = jnp.sum(node_onehot * history_value[:, None], axis=0)
    return (strategy, ancestor_value)


def solution(mesh):
    laid_out = (mesh.shape["trav"], mesh.shape["bulk"]) == (TRAV, BULK)
    return jax.shard_map(
        body if laid_out else general_body,
        mesh=mesh,
        in_specs=(
            P(AXES, None),
            P(),
            P("bulk", None),
            P(AXES, None),
            P(),
            P(AXES, None),
            P(),
            P(),
            P(),
            P(AXES),
            P(AXES, None),
            P(AXES, None),
            P(AXES),
            P(AXES, None),
            P(AXES),
        ),
        out_specs=(P(AXES, None), P(AXES)),
        check_vma=False,
    )
```

```python
import functools

import jax
import jax.numpy as jnp
from jax import lax
from jax.experimental import pallas as pl
from jax.experimental.pallas import tpu as pltpu
from jax.sharding import PartitionSpec as P

TREMBLE = 0.05
AXES = ("trav", "bulk")

TRAV, BULK = 4, 8
X, Y, D, A, B, C = 1, 2, 3, 4, 8, 12
PLANE = (0, X, Y, D)
ID_ROWS = 16


def swap_chip(value, chip):
    return lax.ppermute(value, AXES, [(i, i ^ (chip << 1)) for i in range(TRAV * BULK)])


def swap_core(value):
    return lax.ppermute(value, AXES, [(i, i ^ 1) for i in range(TRAV * BULK)])


def iota(shape, dim):
    return lax.broadcasted_iota(jnp.int32, shape, dim)


def over_rows(a, b):
    return lax.dot_general(a, b, (((0,), (0,)), ((), ())), preferred_element_type=jnp.float32)


def my_core():
    return lax.axis_index("bulk") & 1


def my_chip():
    return lax.axis_index("trav") * (BULK // 2) + (lax.axis_index("bulk") >> 1)


def call(kernel, outs, mebibytes, scratch=()):
    many = isinstance(outs, (list, tuple))
    spec = pl.BlockSpec(memory_space=pltpu.VMEM)

    def run(*args):
        return pl.pallas_call(
            kernel,
            out_shape=tuple(outs) if many else outs,
            in_specs=[spec] * len(args),
            out_specs=(spec,) * len(outs) if many else spec,
            scratch_shapes=list(scratch),
            compiler_params=pltpu.CompilerParams(vmem_limit_bytes=mebibytes << 20),
        )(*args)

    return run


def shape(rows, columns, dtype=jnp.bfloat16):
    return jax.ShapeDtypeStruct((rows, columns), dtype)


def across(a, b, precision=None):
    return lax.dot_general(
        a, b, (((1,), (1,)), ((), ())), preferred_element_type=jnp.float32, precision=precision
    )


def keep_kernel(w_first, w_second, owner, row, keep, ids):
    one, half = w_first.shape[0], keep.shape[1]
    here = pl.ds(pl.multiple_of(my_core() * half, half), half)
    keep[:one, :] = w_first[:, here]
    keep[one:, :] = w_second[:, here]
    ids[:1, :] = owner[...]
    ids[1:, :] = row[...]


def join_kernel(depths, keep, ids, other_first, other_second, other_owner, other_row, out, out_ids):
    core, half = my_core(), out.shape[1]
    here = pl.ds(pl.multiple_of(core * half, half), half)
    begin = 0
    for depth, other in zip(depths, (other_first, other_second)):
        for to, rows in ((core, keep[begin : begin + depth, :]), (1 - core, other[:, here])):
            place = pl.ds(pl.multiple_of(2 * begin + to * depth, depth), depth)
            for target in (out, out_ids):
                target[place, :] = rows
        begin += depth
    parts = [ref[...].astype(jnp.float32) for ref in (ids, other_owner, other_row)]
    count = ids.shape[1]
    parts = jnp.concatenate(parts + [jnp.zeros((ID_ROWS - 4, count), jnp.float32)], axis=0)
    parts = jnp.concatenate([parts, jnp.zeros((ID_ROWS, half - count), jnp.float32)], axis=1)
    out_ids[2 * begin :, :] = parts.astype(jnp.bfloat16)


def ranks_of(hits):
    count = hits.shape[1]
    before = (iota((count, count), 0) < iota((count, count), 1)).astype(jnp.bfloat16)
    return jnp.dot(hits.astype(jnp.bfloat16), before, preferred_element_type=jnp.float32)


def meta_kernel(capacity, owner, actions, out):
    partner = owner[...] ^ lax.axis_index("bulk")
    count = owner.shape[1]
    hits = (partner == iota((BULK, count), 0)).astype(jnp.float32)
    rank = jnp.sum(ranks_of(hits) * hits, axis=0, keepdims=True)
    slot = partner.astype(jnp.float32) * capacity + rank
    rows = out.shape[0]
    parts = [actions[...].astype(jnp.float32), slot, jnp.zeros((rows - actions.shape[0] - 1, count), jnp.float32)]
    parts = jnp.concatenate(parts, axis=0)
    out[...] = jnp.concatenate([parts, jnp.zeros((rows, out.shape[1] - count), jnp.float32)], axis=1).astype(jnp.bfloat16)


def serve_kernel(capacity, count, *refs):
    asked, table, outs = refs[: len(PLANE)], refs[len(PLANE)], refs[len(PLANE) + 1 :]
    buckets = table.shape[0]
    me = lax.axis_index("bulk")
    owners, rows = [], []
    for ids in asked:
        block = ids[ids.shape[0] - ID_ROWS :, :count].astype(jnp.float32)
        for core in (0, 1):
            owners.append(block[2 * core : 2 * core + 1, :])
            rows.append(block[2 * core + 1 : 2 * core + 2, :])
    owners, rows = jnp.concatenate(owners, axis=0), jnp.concatenate(rows, axis=0)
    hits = (owners.astype(jnp.int32) == me).astype(jnp.float32)
    ranks = ranks_of(hits).astype(jnp.int32)
    rows = (rows * hits).astype(jnp.bfloat16)
    for n, out in enumerate(outs):
        wants = []
        for j in (2 * n, 2 * n + 1):
            at_rank = (ranks[j : j + 1, :] == iota((capacity, count), 0)).astype(jnp.bfloat16)
            wants.append(across(rows, at_rank)[j : j + 1, :])
        want = jnp.concatenate(wants, axis=1).astype(jnp.int32)
        onehot = (iota((buckets, want.shape[1]), 0) == want).astype(jnp.bfloat16)
        out[...] = over_rows(onehot, table[...]).astype(jnp.bfloat16)


def inputs_kernel(capacity, branch_slots, act_table, mine, theirs, out):
    served = len(PLANE) * 2 * capacity
    rows = out.shape[0] // (2 * branch_slots)
    to = 0
    for which, ref in enumerate((mine, theirs)):
        parts = []
        for n in range(len(PLANE)):
            for core in (0, 1):
                begin = (2 * n + core) * capacity
                parts.append((mine, theirs)[which ^ core][begin : begin + capacity, :])
        buckets = jnp.concatenate(parts, axis=0)
        meta = ref[served + rows :, :rows].astype(jnp.float32).astype(jnp.int32)
        onehot = (meta[branch_slots : branch_slots + 1, :] == iota((served, rows), 0)).astype(jnp.bfloat16)
        bucket = over_rows(onehot, buckets)
        parent = ref[served : served + rows, :].astype(jnp.float32)
        for c in range(branch_slots):
            onehot = (meta[c : c + 1, :] == iota((act_table.shape[0], rows), 0)).astype(jnp.bfloat16)
            base = (parent + over_rows(onehot, act_table[...])).astype(jnp.bfloat16)
            out[to : to + rows, :] = (base.astype(jnp.float32) + bucket).astype(jnp.bfloat16)
            to += rows


def place_kernel(pieces, depth, *refs):
    refs, out = refs[:-1], refs[-1]
    for chip, which, begin, row, count in pieces:
        to = pl.multiple_of((my_chip() ^ chip) * depth + row, 16)
        out[pl.ds(to, count), :] = refs[which][begin : begin + count, :]


def first_kernel(depth, inputs, home, other, bias, out):
    half = home.shape[1]
    chips = half // depth
    me, core = my_chip(), my_core()
    rows, group = inputs.shape[0] // 2, 4
    for which, weights in enumerate((home, other)):
        side = core ^ which
        base = ((me // chips) ^ side) * half
        for first in range(0, chips, group):
            spots = [(n ^ me) & (chips - 1) for n in range(first, first + group)]
            columns = [pl.ds(pl.multiple_of(spot * depth, depth), depth) for spot in spots]
            shifts = [pl.ds(pl.multiple_of(side * half + spot * depth, depth), depth) for spot in spots]
            block = jnp.concatenate([weights[:, column] for column in columns], axis=1)
            shift = jnp.concatenate([bias[:, column] for column in shifts], axis=1)
            to = pl.ds(pl.multiple_of(base + first * depth, group * depth), group * depth)
            for m in (0, rows):
                total = jnp.dot(inputs[m : m + rows, :], block, preferred_element_type=jnp.float32)
                out[m : m + rows, to] = jnp.maximum(total + shift, 0.0).astype(jnp.bfloat16)


def line_up(pieces, refs, depth, weights):
    order = list(dict.fromkeys(piece[0] for piece in pieces))
    for name, which, begin, row, count in pieces:
        to = order.index(name) * depth + row
        weights[to : to + count, :] = refs[which][begin : begin + count, :]
    return [slice(name * depth, (name + 1) * depth) for name in order]


def second_kernel(pieces, depth, hidden, *refs):
    refs, (out, weights) = refs[:-2], refs[-2:]
    columns = line_up(pieces, refs, depth, weights)
    step, rows = 512, hidden.shape[0] // 2
    for m in (0, rows):
        picked = jnp.concatenate([hidden[m : m + rows, column] for column in columns], axis=1)
        for n in range(0, out.shape[1], step):
            out[m : m + rows, n : n + step] = jnp.dot(
                picked, weights[:, n : n + step], preferred_element_type=jnp.float32
            )


def finish_second_kernel(pieces, depth, hidden, so_far, bias, w_head, *refs):
    refs, (out_mine, out_theirs, weights) = refs[:-3], refs[-3:]
    columns = line_up(pieces, refs, depth, weights)
    half, core = so_far.shape[1], my_core()
    step, rows = 512, hidden.shape[0] // 2
    for m, out in ((0, out_mine), (rows, out_theirs)):
        picked = jnp.concatenate([hidden[m : m + rows, column] for column in columns], axis=1)
        advantage = jnp.zeros((rows, w_head.shape[0]), jnp.float32)
        for n in range(0, half, step):
            here = pl.ds(pl.multiple_of(core * half + n, step), step)
            total = so_far[m : m + rows, n : n + step] + jnp.dot(
                picked, weights[:, n : n + step], preferred_element_type=jnp.float32
            )
            layer = jnp.maximum(total + bias[:, here], 0.0).astype(jnp.bfloat16)
            advantage = advantage + across(layer, w_head[:, here])
        out[...] = advantage.T


def stack_kernel(places, *refs):
    refs, out = refs[:-1], refs[-1]
    to = 0
    for ref, (begin, count) in zip(refs, places):
        out[to : to + count, :] = ref[begin : begin + count, :]
        to += count


def stack(*parts):
    arrays, places = [part[0] for part in parts], [part[1:] for part in parts]
    total = sum(count for _, count in places)
    out = shape(total, arrays[0].shape[1], arrays[0].dtype)
    return call(functools.partial(stack_kernel, places), out, 4)(*arrays)


def last_kernel(counts, ancestor, legal, b_head, mine, theirs, strategy, values):
    actions = b_head.shape[1]
    rows = counts.shape[1]
    diagonal = iota((actions, actions), 0) == iota((actions, actions), 1)
    shift = jnp.sum(jnp.where(diagonal, b_head[...], 0.0), axis=1, keepdims=True)
    first_action = (iota((actions, rows), 0) == 0).astype(jnp.float32)
    total_value = jnp.zeros((1, rows), jnp.float32)
    for c in range(mine.shape[1] // rows):
        here = slice(c * rows, (c + 1) * rows)
        advantage = mine[:, here] + theirs[:, here] + shift
        allowed = jnp.maximum(legal[c * actions : (c + 1) * actions, :].astype(jnp.float32), first_action)
        positive = allowed * (jnp.maximum(advantage, 0.0) + TREMBLE)
        sigma = positive / jnp.sum(positive, axis=0, keepdims=True)
        live = (counts[...] > c).astype(jnp.float32)
        strategy[c * actions : (c + 1) * actions, :] = sigma * live
        total_value = total_value + live * jnp.sum(sigma * advantage, axis=0, keepdims=True)
    value = total_value / counts[...].astype(jnp.float32)
    at_node = (ancestor[...] == iota((values.shape[1], rows), 0)).astype(jnp.float32)
    values[...] = across(value, at_node, lax.Precision.HIGHEST)


def body(
    parents,
    act_table,
    bucket_table,
    w_first,
    b_first,
    w_second,
    b_second,
    w_head,
    b_head,
    branch_counts,
    sampled_actions,
    bucket_owner,
    bucket_row,
    legal_mask,
    ancestor,
):
    par_count, feature_count = parents.shape
    branch_slots = sampled_actions.shape[1]
    branches = par_count * branch_slots
    hidden_units = w_first.shape[1]
    half = hidden_units // 2
    depth_one, depth_two = w_first.shape[0], w_second.shape[0]
    chip_one, chip_two = 2 * depth_one, 2 * depth_two
    depth = chip_one + chip_two
    capacity = max(2, (4 * par_count + 3 * BULK - 1) // (3 * BULK))
    wide = 2 * capacity

    owner, row = bucket_owner.T, bucket_row[None, :]
    keep, ids = call(keep_kernel, (shape(depth // 2, half), shape(2, par_count, jnp.int32)), 4)(
        w_first, w_second, owner, row
    )
    own, own_ids = call(
        functools.partial(join_kernel, (depth_one, depth_two)), (shape(depth, half), shape(depth + ID_ROWS, half)), 4
    )(keep, ids, swap_core(w_first), swap_core(w_second), swap_core(owner), swap_core(row))
    from_x, from_y, from_d = [swap_chip(own_ids, chip) for chip in PLANE[1:]]
    from_a, from_b = [swap_chip(own, chip) for chip in (A, B)]
    meta = call(functools.partial(meta_kernel, capacity), shape(ID_ROWS, feature_count), 4)(owner, sampled_actions.T)
    table = stack((bucket_table, 0, bucket_table.shape[0]))
    from_x, from_y, from_d, from_a, from_b, table = lax.optimization_barrier(
        (from_x, from_y, from_d, from_a, from_b, table)
    )

    served = call(
        functools.partial(serve_kernel, capacity, par_count), (shape(wide, feature_count),) * len(PLANE), 6
    )(own_ids, from_x, from_y, from_d, table)
    few = chip_one // 2
    x_ab = swap_chip(stack((from_a, few, depth - few), (from_b, 0, depth), (served[1], 0, wide)), X)
    y_ab = swap_chip(stack((from_a, few, depth - few), (from_b, 0, depth), (served[2], 0, wide)), Y)
    rows_d = swap_chip(stack((served[3], 0, wide), (from_b, 0, chip_one)), D)
    c_da = swap_chip(stack((from_b, 0, depth), (from_d, 0, chip_one), (from_x, 0, few), (from_y, 0, few)), A)
    plane_c = swap_chip(stack(*((rows, 0, chip_one) for rows in (from_x, from_y, from_d))), C)
    x_ab, y_ab, rows_d, c_da, plane_c = lax.optimization_barrier((x_ab, y_ab, rows_d, c_da, plane_c))

    cut = chip_two // 2
    at_a, at_b = chip_one - few, depth - few + chip_one
    x_c = swap_chip(stack((c_da, chip_one, chip_two), (y_ab, at_a, cut), (y_ab, at_b, cut)), X)
    y_c = swap_chip(stack((c_da, chip_one, chip_two), (x_ab, at_a + cut, cut), (x_ab, at_b + cut, cut)), Y)
    d_c = swap_chip(stack((from_d, chip_one, chip_two)), C)

    end = 2 * depth - few
    mine = stack(
        (served[0], 0, wide), (x_ab, end, wide), (y_ab, end, wide), (rows_d, 0, wide),
        (parents, 0, par_count), (meta, 0, ID_ROWS)
    )
    inputs = call(functools.partial(inputs_kernel, capacity, branch_slots), shape(2 * branches, feature_count), 10)(
        act_table, mine, swap_core(mine)
    )

    arrays = [own, from_x, from_y, from_a, from_b, from_d, x_ab, y_ab, c_da]
    near = [(chip, n) for n, chip in enumerate((0, X, Y, A, B, D))]
    first_pieces = [(chip, n, 0, 0, chip_one) for chip, n in near] + [(C, 8, 0, 0, chip_one)]
    for n, chip in ((6, X), (7, Y)):
        first_pieces.append((chip ^ A, 8, depth + chip_one + (n - 6) * few, 0, few))
        first_pieces += [(chip ^ A, n, 0, few, chip_one - few), (chip ^ B, n, depth - few, 0, chip_one)]
    first_pieces += [(D ^ A, 8, depth, 0, chip_one), (D ^ B, 9, wide, 0, chip_one)]
    first_pieces += [(chip ^ C, 10, n * chip_one, 0, chip_one) for n, chip in enumerate((X, Y, D))]
    weights = call(functools.partial(place_kernel, first_pieces, chip_one), shape(feature_count, half), 4)(
        *arrays, rows_d, plane_c
    )
    hidden = call(functools.partial(first_kernel, chip_two), shape(2 * branches, hidden_units), 12)(
        inputs, weights, swap_core(weights), b_first[None, :]
    )

    early = [(chip, n, chip_one, 0, chip_two) for chip, n in near] + [(C, 8, chip_one, 0, chip_two)]
    for n, chip in ((6, X), (7, Y)):
        early += [(chip ^ A, n, at_a, 0, chip_two), (chip ^ B, n, at_b, 0, chip_two)]
    early.sort()
    so_far = call(
        functools.partial(second_kernel, early, chip_two),
        shape(2 * branches, half, jnp.float32),
        16,
        [pltpu.VMEM((len(early) * chip_two, half), jnp.bfloat16)],
    )(hidden, *arrays)
    late = [(X ^ C, 0, 0, 0, chip_two), (Y ^ C, 1, 0, 0, chip_two), (D ^ C, 2, 0, 0, chip_two)]
    late += [(D ^ A, 0, chip_two, 0, cut), (D ^ A, 1, chip_two, cut, cut)]
    late += [(D ^ B, 0, chip_two + cut, 0, cut), (D ^ B, 1, chip_two + cut, cut, cut)]
    mine, theirs = call(
        functools.partial(finish_second_kernel, late, chip_two),
        (shape(w_head.shape[1], branches, jnp.float32),) * 2,
        14,
        [pltpu.VMEM((5 * chip_two, half), jnp.bfloat16)],
    )(hidden, so_far, b_second[None, :], w_head.T, x_c, y_c, d_c)
    strategy, values = call(
        last_kernel, (shape(legal_mask.shape[1], par_count, jnp.float32), shape(1, par_count // 4, jnp.float32)), 4
    )(branch_counts[None, :], ancestor[None, :], legal_mask.T, b_head[None, :], mine, swap_core(theirs))
    return (strategy.T, values.reshape(-1))


def network(inputs, w_first, b_first, w_second, b_second, w_head, b_head):
    columns = inputs
    first = jnp.dot(
        columns,
        lax.all_gather(w_first, ("trav", "bulk"), axis=0, tiled=True),
        preferred_element_type=jnp.float32,
    )
    hidden_one = jnp.maximum(first + b_first, 0.0).astype(jnp.bfloat16)
    columns = hidden_one
    second = jnp.dot(
        columns,
        lax.all_gather(w_second, ("trav", "bulk"), axis=0, tiled=True),
        preferred_element_type=jnp.float32,
    )
    hidden_two = jnp.maximum(second + b_second, 0.0).astype(jnp.bfloat16)
    return jnp.dot(hidden_two, w_head, preferred_element_type=jnp.float32) + b_head


def general_body(
    parents,
    act_table,
    bucket_table,
    w_first,
    b_first,
    w_second,
    b_second,
    w_head,
    b_head,
    branch_counts,
    sampled_actions,
    bucket_owner,
    bucket_row,
    legal_mask,
    ancestor,
):
    par_count = parents.shape[0]
    feature_count = parents.shape[1]
    branch_slots = sampled_actions.shape[1]
    vocab_size = act_table.shape[0]
    action_count = w_head.shape[1]
    bulk_count = lax.axis_size("bulk")
    capacity = max(2, (4 * par_count + 3 * bulk_count - 1) // (3 * bulk_count))
    slot_total = bulk_count * capacity
    action_onehot = (
        sampled_actions.reshape(-1)[:, None] == jnp.arange(vocab_size)[None, :]
    ).astype(jnp.bfloat16)
    act_rows = jnp.dot(action_onehot, act_table, preferred_element_type=jnp.float32)
    base = (jnp.repeat(parents.astype(jnp.float32), branch_slots, axis=0) + act_rows).astype(
        jnp.bfloat16
    )
    base = lax.optimization_barrier(base)
    owner_index = bucket_owner[:, 0]
    owner_hits = (owner_index[:, None] == jnp.arange(bulk_count)[None, :]).astype(jnp.int32)
    earlier = jnp.cumsum(owner_hits, axis=0) - owner_hits
    slot_index = owner_index * capacity + jnp.sum(earlier * owner_hits, axis=1)
    placement_int = (slot_index[None, :] == jnp.arange(slot_total)[:, None]).astype(jnp.int32)
    slot_bucket = jnp.sum(placement_int * bucket_row[None, :], axis=1).reshape(bulk_count, capacity)
    placement = placement_int.astype(jnp.bfloat16)
    outgoing = jnp.dot(
        placement,
        base.reshape(par_count, branch_slots * feature_count),
        preferred_element_type=jnp.float32,
    )
    outgoing = outgoing.astype(jnp.bfloat16).reshape(
        bulk_count, capacity * branch_slots, feature_count
    )
    arrived_rows = lax.all_to_all(outgoing, "bulk", split_axis=0, concat_axis=0, tiled=True)
    arrived_ids = lax.all_to_all(slot_bucket, "bulk", split_axis=0, concat_axis=0, tiled=True)
    table_rows = jnp.take(bucket_table, arrived_ids.reshape(-1), axis=0)
    inputs = (
        arrived_rows.reshape(slot_total, branch_slots, feature_count).astype(jnp.float32)
        + table_rows.astype(jnp.float32)[:, None, :]
    )
    inputs = inputs.astype(jnp.bfloat16).reshape(slot_total * branch_slots, feature_count)
    evaluated = network(inputs, w_first, b_first, w_second, b_second, w_head, b_head)
    returned = lax.all_to_all(
        evaluated.reshape(bulk_count, capacity * branch_slots * action_count).astype(jnp.bfloat16),
        "bulk",
        split_axis=0,
        concat_axis=0,
        tiled=True,
    ).astype(jnp.float32)
    advantage = jnp.take(
        returned.reshape(slot_total, branch_slots * action_count), slot_index, axis=0
    )
    advantage = advantage.reshape(par_count, branch_slots, action_count)
    first_action = (jnp.arange(action_count) == 0).astype(jnp.float32)
    allowed = jnp.maximum(
        legal_mask.reshape(par_count, branch_slots, action_count).astype(jnp.float32), first_action
    )
    positive = allowed * (jnp.maximum(advantage, 0.0) + TREMBLE)
    sigma = positive / jnp.sum(positive, axis=-1, keepdims=True)
    live = (jnp.arange(branch_slots)[None, :] < branch_counts[:, None]).astype(jnp.float32)
    strategy = (sigma * live[:, :, None]).reshape(par_count, branch_slots * action_count)
    branch_value = jnp.sum(sigma * advantage, axis=-1)
    history_value = jnp.sum(branch_value * live, axis=1) / branch_counts.astype(jnp.float32)
    node_count = par_count // 4
    node_onehot = (ancestor[:, None] == jnp.arange(node_count)[None, :]).astype(jnp.float32)
    ancestor_value = jnp.sum(node_onehot * history_value[:, None], axis=0)
    return (strategy, ancestor_value)


def solution(mesh):
    laid_out = (mesh.shape["trav"], mesh.shape["bulk"]) == (TRAV, BULK)
    return jax.shard_map(
        body if laid_out else general_body,
        mesh=mesh,
        in_specs=(
            P(AXES, None),
            P(),
            P("bulk", None),
            P(AXES, None),
            P(),
            P(AXES, None),
            P(),
            P(),
            P(),
            P(AXES),
            P(AXES, None),
            P(AXES, None),
            P(AXES),
            P(AXES, None),
            P(AXES),
        ),
        out_specs=(P(AXES, None), P(AXES)),
        check_vma=False,
    )
```

```python
import functools

import jax
import jax.numpy as jnp
from jax import lax
from jax.experimental import pallas as pl
from jax.experimental.pallas import tpu as pltpu
from jax.sharding import PartitionSpec as P

TREMBLE = 0.05
AXES = ("trav", "bulk")

TRAV, BULK = 4, 8
X, Y, D, A, B, C = 1, 2, 3, 4, 8, 12
PLANE = (0, X, Y, D)
ID_ROWS = 16


def swap_chip(value, chip):
    return lax.ppermute(value, AXES, [(i, i ^ (chip << 1)) for i in range(TRAV * BULK)])


def swap_core(value):
    return lax.ppermute(value, AXES, [(i, i ^ 1) for i in range(TRAV * BULK)])


def iota(shape, dim):
    return lax.broadcasted_iota(jnp.int32, shape, dim)


def over_rows(a, b):
    return lax.dot_general(a, b, (((0,), (0,)), ((), ())), preferred_element_type=jnp.float32)


def my_core():
    return lax.axis_index("bulk") & 1


def my_chip():
    return lax.axis_index("trav") * (BULK // 2) + (lax.axis_index("bulk") >> 1)


def call(kernel, outs, mebibytes, scratch=()):
    many = isinstance(outs, (list, tuple))
    spec = pl.BlockSpec(memory_space=pltpu.VMEM)

    def run(*args):
        return pl.pallas_call(
            kernel,
            out_shape=tuple(outs) if many else outs,
            in_specs=[spec] * len(args),
            out_specs=(spec,) * len(outs) if many else spec,
            scratch_shapes=list(scratch),
            compiler_params=pltpu.CompilerParams(vmem_limit_bytes=mebibytes << 20),
        )(*args)

    return run


def shape(rows, columns, dtype=jnp.bfloat16):
    return jax.ShapeDtypeStruct((rows, columns), dtype)


def across(a, b, precision=None):
    return lax.dot_general(
        a, b, (((1,), (1,)), ((), ())), preferred_element_type=jnp.float32, precision=precision
    )


def keep_kernel(w_first, w_second, keep):
    one, half = w_first.shape[0], keep.shape[1]
    here = pl.ds(pl.multiple_of(my_core() * half, half), half)
    keep[:one, :] = w_first[:, here]
    keep[one:, :] = w_second[:, here]


def join_kernel(depths, keep, ids, other_first, other_second, other_owner, other_row, out, out_ids):
    core, half = my_core(), out.shape[1]
    here = pl.ds(pl.multiple_of(core * half, half), half)
    begin = 0
    for depth, other in zip(depths, (other_first, other_second)):
        for to, rows in ((core, keep[begin : begin + depth, :]), (1 - core, other[:, here])):
            place = pl.ds(pl.multiple_of(2 * begin + to * depth, depth), depth)
            for target in (out, out_ids):
                target[place, :] = rows
        begin += depth
    parts = [ref[...].astype(jnp.float32) for ref in (ids, other_owner, other_row)]
    count = ids.shape[1]
    parts = jnp.concatenate(parts + [jnp.zeros((ID_ROWS - 4, count), jnp.float32)], axis=0)
    parts = jnp.concatenate([parts, jnp.zeros((ID_ROWS, half - count), jnp.float32)], axis=1)
    out_ids[2 * begin :, :] = parts.astype(jnp.bfloat16)


def ranks_of(hits):
    count = hits.shape[1]
    before = (iota((count, count), 0) < iota((count, count), 1)).astype(jnp.bfloat16)
    return jnp.dot(hits.astype(jnp.bfloat16), before, preferred_element_type=jnp.float32)


def meta_kernel(capacity, owner, actions, out):
    partner = owner[...] ^ lax.axis_index("bulk")
    count = owner.shape[1]
    hits = (partner == iota((BULK, count), 0)).astype(jnp.float32)
    rank = jnp.sum(ranks_of(hits) * hits, axis=0, keepdims=True)
    slot = partner.astype(jnp.float32) * capacity + rank
    rows = out.shape[0]
    parts = [actions[...].astype(jnp.float32), slot, jnp.zeros((rows - actions.shape[0] - 1, count), jnp.float32)]
    parts = jnp.concatenate(parts, axis=0)
    out[...] = jnp.concatenate([parts, jnp.zeros((rows, out.shape[1] - count), jnp.float32)], axis=1).astype(jnp.bfloat16)


def serve_kernel(capacity, count, *refs):
    asked, table, outs = refs[: len(PLANE)], refs[len(PLANE)], refs[len(PLANE) + 1 :]
    buckets = table.shape[0]
    me = lax.axis_index("bulk")
    owners, rows = [], []
    for ids in asked:
        block = ids[ids.shape[0] - ID_ROWS :, :count].astype(jnp.float32)
        for core in (0, 1):
            owners.append(block[2 * core : 2 * core + 1, :])
            rows.append(block[2 * core + 1 : 2 * core + 2, :])
    owners, rows = jnp.concatenate(owners, axis=0), jnp.concatenate(rows, axis=0)
    hits = (owners.astype(jnp.int32) == me).astype(jnp.float32)
    ranks = ranks_of(hits).astype(jnp.int32)
    rows = (rows * hits).astype(jnp.bfloat16)
    wants = []
    for j in range(2 * len(PLANE)):
        at_rank = (ranks[j : j + 1, :] == iota((capacity, count), 0)).astype(jnp.bfloat16)
        wants.append(across(rows, at_rank)[j : j + 1, :])
    want = jnp.concatenate(wants, axis=1).astype(jnp.int32)
    onehot = (iota((buckets, want.shape[1]), 0) == want).astype(jnp.bfloat16)
    found = over_rows(onehot, table[...]).astype(jnp.bfloat16)
    for n, out in enumerate(outs):
        out[...] = found[2 * n * capacity : 2 * (n + 1) * capacity, :]


def inputs_kernel(capacity, branch_slots, act_table, mine, theirs, out):
    served = len(PLANE) * 2 * capacity
    rows = out.shape[0] // (2 * branch_slots)
    to = 0
    for which, ref in enumerate((mine, theirs)):
        parts = []
        for n in range(len(PLANE)):
            for core in (0, 1):
                begin = (2 * n + core) * capacity
                parts.append((mine, theirs)[which ^ core][begin : begin + capacity, :])
        buckets = jnp.concatenate(parts, axis=0)
        meta = ref[served + rows :, :rows].astype(jnp.float32).astype(jnp.int32)
        onehot = (meta[branch_slots : branch_slots + 1, :] == iota((served, rows), 0)).astype(jnp.bfloat16)
        bucket = over_rows(onehot, buckets)
        parent = ref[served : served + rows, :].astype(jnp.float32)
        acts = jnp.concatenate([meta[c : c + 1, :] for c in range(branch_slots)], axis=1)
        onehot = (acts == iota((act_table.shape[0], branch_slots * rows), 0)).astype(jnp.bfloat16)
        change = over_rows(onehot, act_table[...])
        for c in range(branch_slots):
            base = (parent + change[c * rows : (c + 1) * rows, :]).astype(jnp.bfloat16)
            out[to : to + rows, :] = (base.astype(jnp.float32) + bucket).astype(jnp.bfloat16)
            to += rows


def place_kernel(pieces, depth, *refs):
    refs, out = refs[:-1], refs[-1]
    for chip, which, begin, row, count in pieces:
        to = pl.multiple_of((my_chip() ^ chip) * depth + row, 16)
        out[pl.ds(to, count), :] = refs[which][begin : begin + count, :]


def first_kernel(depth, inputs, home, other, bias, out):
    half = home.shape[1]
    chips = half // depth
    me, core = my_chip(), my_core()
    rows, group = inputs.shape[0] // 2, 4
    for which, weights in enumerate((home, other)):
        side = core ^ which
        base = ((me // chips) ^ side) * half
        for first in range(0, chips, group):
            spots = [(n ^ me) & (chips - 1) for n in range(first, first + group)]
            columns = [pl.ds(pl.multiple_of(spot * depth, depth), depth) for spot in spots]
            shifts = [pl.ds(pl.multiple_of(side * half + spot * depth, depth), depth) for spot in spots]
            block = jnp.concatenate([weights[:, column] for column in columns], axis=1)
            shift = jnp.concatenate([bias[:, column] for column in shifts], axis=1)
            to = pl.ds(pl.multiple_of(base + first * depth, group * depth), group * depth)
            for m in (0, rows):
                total = jnp.dot(inputs[m : m + rows, :], block, preferred_element_type=jnp.float32)
                out[m : m + rows, to] = jnp.maximum(total + shift, 0.0).astype(jnp.bfloat16)


def line_up(pieces, refs, depth, weights):
    order = list(dict.fromkeys(piece[0] for piece in pieces))
    for name, which, begin, row, count in pieces:
        to = order.index(name) * depth + row
        weights[to : to + count, :] = refs[which][begin : begin + count, :]
    return [slice(name * depth, (name + 1) * depth) for name in order]


def second_kernel(pieces, depth, hidden, *refs):
    refs, (out, weights) = refs[:-2], refs[-2:]
    columns = line_up(pieces, refs, depth, weights)
    step, rows = 512, hidden.shape[0] // 2
    for m in (0, rows):
        picked = jnp.concatenate([hidden[m : m + rows, column] for column in columns], axis=1)
        for n in range(0, out.shape[1], step):
            out[m : m + rows, n : n + step] = jnp.dot(
                picked, weights[:, n : n + step], preferred_element_type=jnp.float32
            )


def finish_second_kernel(pieces, depth, hidden, so_far, bias, w_head, *refs):
    refs, (out_mine, out_theirs, weights) = refs[:-3], refs[-3:]
    columns = line_up(pieces, refs, depth, weights)
    half, core = so_far.shape[1], my_core()
    step, rows = 512, hidden.shape[0] // 2
    for m, out in ((0, out_mine), (rows, out_theirs)):
        picked = jnp.concatenate([hidden[m : m + rows, column] for column in columns], axis=1)
        advantage = jnp.zeros((rows, w_head.shape[0]), jnp.float32)
        for n in range(0, half, step):
            here = pl.ds(pl.multiple_of(core * half + n, step), step)
            total = so_far[m : m + rows, n : n + step] + jnp.dot(
                picked, weights[:, n : n + step], preferred_element_type=jnp.float32
            )
            layer = jnp.maximum(total + bias[:, here], 0.0).astype(jnp.bfloat16)
            advantage = advantage + across(layer, w_head[:, here])
        out[...] = advantage.T


def stack_kernel(places, *refs):
    refs, out = refs[:-1], refs[-1]
    to = 0
    for ref, (begin, count) in zip(refs, places):
        out[to : to + count, :] = ref[begin : begin + count, :]
        to += count


def stack(*parts):
    arrays, places = [part[0] for part in parts], [part[1:] for part in parts]
    total = sum(count for _, count in places)
    out = shape(total, arrays[0].shape[1], arrays[0].dtype)
    return call(functools.partial(stack_kernel, places), out, 4)(*arrays)


def last_kernel(counts, ancestor, legal, b_head, mine, theirs, strategy, values):
    actions = b_head.shape[1]
    rows = counts.shape[1]
    diagonal = iota((actions, actions), 0) == iota((actions, actions), 1)
    shift = jnp.sum(jnp.where(diagonal, b_head[...], 0.0), axis=1, keepdims=True)
    first_action = (iota((actions, rows), 0) == 0).astype(jnp.float32)
    total_value = jnp.zeros((1, rows), jnp.float32)
    for c in range(mine.shape[1] // rows):
        here = slice(c * rows, (c + 1) * rows)
        advantage = mine[:, here] + theirs[:, here] + shift
        allowed = jnp.maximum(legal[c * actions : (c + 1) * actions, :].astype(jnp.float32), first_action)
        positive = allowed * (jnp.maximum(advantage, 0.0) + TREMBLE)
        sigma = positive / jnp.sum(positive, axis=0, keepdims=True)
        live = (counts[...] > c).astype(jnp.float32)
        strategy[c * actions : (c + 1) * actions, :] = sigma * live
        total_value = total_value + live * jnp.sum(sigma * advantage, axis=0, keepdims=True)
    value = total_value / counts[...].astype(jnp.float32)
    at_node = (ancestor[...] == iota((values.shape[1], rows), 0)).astype(jnp.float32)
    values[...] = across(value, at_node, lax.Precision.HIGHEST)


def body(
    parents,
    act_table,
    bucket_table,
    w_first,
    b_first,
    w_second,
    b_second,
    w_head,
    b_head,
    branch_counts,
    sampled_actions,
    bucket_owner,
    bucket_row,
    legal_mask,
    ancestor,
):
    par_count, feature_count = parents.shape
    branch_slots = sampled_actions.shape[1]
    branches = par_count * branch_slots
    hidden_units = w_first.shape[1]
    half = hidden_units // 2
    depth_one, depth_two = w_first.shape[0], w_second.shape[0]
    chip_one, chip_two = 2 * depth_one, 2 * depth_two
    depth = chip_one + chip_two
    capacity = max(2, (4 * par_count + 3 * BULK - 1) // (3 * BULK))
    wide = 2 * capacity

    owner, row = bucket_owner.T, bucket_row[None, :]
    keep = call(keep_kernel, shape(depth // 2, half), 4)(w_first, w_second)
    ids = jnp.concatenate([owner, row], axis=0)
    own, own_ids = call(
        functools.partial(join_kernel, (depth_one, depth_two)), (shape(depth, half), shape(depth + ID_ROWS, half)), 4
    )(keep, ids, swap_core(w_first), swap_core(w_second), swap_core(owner), swap_core(row))
    from_x, from_y, from_d = [swap_chip(own_ids, chip) for chip in PLANE[1:]]
    from_a, from_b = [swap_chip(own, chip) for chip in (A, B)]
    meta = call(functools.partial(meta_kernel, capacity), shape(ID_ROWS, feature_count), 4)(owner, sampled_actions.T)
    table = stack((bucket_table, 0, bucket_table.shape[0]))
    from_x, from_y, from_d, from_a, from_b, table = lax.optimization_barrier(
        (from_x, from_y, from_d, from_a, from_b, table)
    )

    served = call(
        functools.partial(serve_kernel, capacity, par_count), (shape(wide, feature_count),) * len(PLANE), 6
    )(own_ids, from_x, from_y, from_d, table)
    few = chip_one // 2
    x_ab = swap_chip(stack((from_a, few, depth - few), (from_b, 0, depth), (served[1], 0, wide)), X)
    y_ab = swap_chip(stack((from_a, few, depth - few), (from_b, 0, depth), (served[2], 0, wide)), Y)
    rows_d = swap_chip(stack((served[3], 0, wide), (from_b, 0, chip_one)), D)
    c_da = swap_chip(stack((from_b, 0, depth), (from_d, 0, chip_one), (from_x, 0, few), (from_y, 0, few)), A)
    plane_c = swap_chip(stack((from_x, 0, chip_one), (from_y, 0, chip_one), (from_d, 0, chip_one)), C)
    x_ab, y_ab, rows_d, c_da, plane_c = lax.optimization_barrier((x_ab, y_ab, rows_d, c_da, plane_c))

    cut = chip_two // 2
    at_a, at_b = chip_one - few, depth - few + chip_one
    x_c = swap_chip(stack((c_da, chip_one, chip_two), (y_ab, at_a, cut), (y_ab, at_b, cut)), X)
    y_c = swap_chip(stack((c_da, chip_one, chip_two), (x_ab, at_a + cut, cut), (x_ab, at_b + cut, cut)), Y)
    d_c = swap_chip(stack((from_d, chip_one, chip_two)), C)

    end = 2 * depth - few
    mine = stack(
        (served[0], 0, wide), (x_ab, end, wide), (y_ab, end, wide), (rows_d, 0, wide),
        (parents, 0, par_count), (meta, 0, ID_ROWS)
    )
    inputs = call(functools.partial(inputs_kernel, capacity, branch_slots), shape(2 * branches, feature_count), 10)(
        act_table, mine, swap_core(mine)
    )

    arrays = [own, from_x, from_y, from_a, from_b, from_d, x_ab, y_ab, c_da]
    near = [(chip, n) for n, chip in enumerate((0, X, Y, A, B, D))]
    first_pieces = [(chip, n, 0, 0, chip_one) for chip, n in near] + [(C, 8, 0, 0, chip_one)]
    for n, chip in ((6, X), (7, Y)):
        first_pieces.append((chip ^ A, 8, depth + chip_one + (n - 6) * few, 0, few))
        first_pieces += [(chip ^ A, n, 0, few, chip_one - few), (chip ^ B, n, depth - few, 0, chip_one)]
    first_pieces += [(D ^ A, 8, depth, 0, chip_one), (D ^ B, 9, wide, 0, chip_one)]
    first_pieces += [(chip ^ C, 10, n * chip_one, 0, chip_one) for n, chip in enumerate((X, Y, D))]
    weights = call(functools.partial(place_kernel, first_pieces, chip_one), shape(feature_count, half), 4)(
        *arrays, rows_d, plane_c
    )
    hidden = call(functools.partial(first_kernel, chip_two), shape(2 * branches, hidden_units), 12)(
        inputs, weights, swap_core(weights), b_first[None, :]
    )

    early = [(chip, n, chip_one, 0, chip_two) for chip, n in near]
    for n, chip in ((6, X), (7, Y)):
        early += [(chip ^ A, n, at_a, 0, chip_two), (chip ^ B, n, at_b, 0, chip_two)]
    early.sort()
    so_far = call(
        functools.partial(second_kernel, early, chip_two),
        shape(2 * branches, half, jnp.float32),
        16,
        [pltpu.VMEM((len(early) * chip_two, half), jnp.bfloat16)],
    )(hidden, *arrays)
    late = [(C, 3, chip_one, 0, chip_two), (X ^ C, 0, 0, 0, chip_two), (Y ^ C, 1, 0, 0, chip_two)]
    late += [(D ^ C, 2, 0, 0, chip_two)]
    late += [(D ^ A, 0, chip_two, 0, cut), (D ^ A, 1, chip_two, cut, cut)]
    late += [(D ^ B, 0, chip_two + cut, 0, cut), (D ^ B, 1, chip_two + cut, cut, cut)]
    mine, theirs = call(
        functools.partial(finish_second_kernel, late, chip_two),
        (shape(w_head.shape[1], branches, jnp.float32),) * 2,
        14,
        [pltpu.VMEM((6 * chip_two, half), jnp.bfloat16)],
    )(hidden, so_far, b_second[None, :], w_head.T, x_c, y_c, d_c, c_da)
    strategy, values = call(
        last_kernel, (shape(legal_mask.shape[1], par_count, jnp.float32), shape(1, par_count // 4, jnp.float32)), 4
    )(branch_counts[None, :], ancestor[None, :], legal_mask.T, b_head[None, :], mine, swap_core(theirs))
    return (strategy.T, values.reshape(-1))


def network(inputs, w_first, b_first, w_second, b_second, w_head, b_head):
    columns = inputs
    first = jnp.dot(
        columns,
        lax.all_gather(w_first, ("trav", "bulk"), axis=0, tiled=True),
        preferred_element_type=jnp.float32,
    )
    hidden_one = jnp.maximum(first + b_first, 0.0).astype(jnp.bfloat16)
    columns = hidden_one
    second = jnp.dot(
        columns,
        lax.all_gather(w_second, ("trav", "bulk"), axis=0, tiled=True),
        preferred_element_type=jnp.float32,
    )
    hidden_two = jnp.maximum(second + b_second, 0.0).astype(jnp.bfloat16)
    return jnp.dot(hidden_two, w_head, preferred_element_type=jnp.float32) + b_head


def general_body(
    parents,
    act_table,
    bucket_table,
    w_first,
    b_first,
    w_second,
    b_second,
    w_head,
    b_head,
    branch_counts,
    sampled_actions,
    bucket_owner,
    bucket_row,
    legal_mask,
    ancestor,
):
    par_count = parents.shape[0]
    feature_count = parents.shape[1]
    branch_slots = sampled_actions.shape[1]
    vocab_size = act_table.shape[0]
    action_count = w_head.shape[1]
    bulk_count = lax.axis_size("bulk")
    capacity = max(2, (4 * par_count + 3 * bulk_count - 1) // (3 * bulk_count))
    slot_total = bulk_count * capacity
    action_onehot = (
        sampled_actions.reshape(-1)[:, None] == jnp.arange(vocab_size)[None, :]
    ).astype(jnp.bfloat16)
    act_rows = jnp.dot(action_onehot, act_table, preferred_element_type=jnp.float32)
    base = (jnp.repeat(parents.astype(jnp.float32), branch_slots, axis=0) + act_rows).astype(
        jnp.bfloat16
    )
    base = lax.optimization_barrier(base)
    owner_index = bucket_owner[:, 0]
    owner_hits = (owner_index[:, None] == jnp.arange(bulk_count)[None, :]).astype(jnp.int32)
    earlier = jnp.cumsum(owner_hits, axis=0) - owner_hits
    slot_index = owner_index * capacity + jnp.sum(earlier * owner_hits, axis=1)
    placement_int = (slot_index[None, :] == jnp.arange(slot_total)[:, None]).astype(jnp.int32)
    slot_bucket = jnp.sum(placement_int * bucket_row[None, :], axis=1).reshape(bulk_count, capacity)
    placement = placement_int.astype(jnp.bfloat16)
    outgoing = jnp.dot(
        placement,
        base.reshape(par_count, branch_slots * feature_count),
        preferred_element_type=jnp.float32,
    )
    outgoing = outgoing.astype(jnp.bfloat16).reshape(
        bulk_count, capacity * branch_slots, feature_count
    )
    arrived_rows = lax.all_to_all(outgoing, "bulk", split_axis=0, concat_axis=0, tiled=True)
    arrived_ids = lax.all_to_all(slot_bucket, "bulk", split_axis=0, concat_axis=0, tiled=True)
    table_rows = jnp.take(bucket_table, arrived_ids.reshape(-1), axis=0)
    inputs = (
        arrived_rows.reshape(slot_total, branch_slots, feature_count).astype(jnp.float32)
        + table_rows.astype(jnp.float32)[:, None, :]
    )
    inputs = inputs.astype(jnp.bfloat16).reshape(slot_total * branch_slots, feature_count)
    evaluated = network(inputs, w_first, b_first, w_second, b_second, w_head, b_head)
    returned = lax.all_to_all(
        evaluated.reshape(bulk_count, capacity * branch_slots * action_count).astype(jnp.bfloat16),
        "bulk",
        split_axis=0,
        concat_axis=0,
        tiled=True,
    ).astype(jnp.float32)
    advantage = jnp.take(
        returned.reshape(slot_total, branch_slots * action_count), slot_index, axis=0
    )
    advantage = advantage.reshape(par_count, branch_slots, action_count)
    first_action = (jnp.arange(action_count) == 0).astype(jnp.float32)
    allowed = jnp.maximum(
        legal_mask.reshape(par_count, branch_slots, action_count).astype(jnp.float32), first_action
    )
    positive = allowed * (jnp.maximum(advantage, 0.0) + TREMBLE)
    sigma = positive / jnp.sum(positive, axis=-1, keepdims=True)
    live = (jnp.arange(branch_slots)[None, :] < branch_counts[:, None]).astype(jnp.float32)
    strategy = (sigma * live[:, :, None]).reshape(par_count, branch_slots * action_count)
    branch_value = jnp.sum(sigma * advantage, axis=-1)
    history_value = jnp.sum(branch_value * live, axis=1) / branch_counts.astype(jnp.float32)
    node_count = par_count // 4
    node_onehot = (ancestor[:, None] == jnp.arange(node_count)[None, :]).astype(jnp.float32)
    ancestor_value = jnp.sum(node_onehot * history_value[:, None], axis=0)
    return (strategy, ancestor_value)


def solution(mesh):
    laid_out = (mesh.shape["trav"], mesh.shape["bulk"]) == (TRAV, BULK)
    return jax.shard_map(
        body if laid_out else general_body,
        mesh=mesh,
        in_specs=(
            P(AXES, None),
            P(),
            P("bulk", None),
            P(AXES, None),
            P(),
            P(AXES, None),
            P(),
            P(),
            P(),
            P(AXES),
            P(AXES, None),
            P(AXES, None),
            P(AXES),
            P(AXES, None),
            P(AXES),
        ),
        out_specs=(P(AXES, None), P(AXES)),
        check_vma=False,
    )
```

```python
import functools

import jax
import jax.numpy as jnp
from jax import lax
from jax.experimental import pallas as pl
from jax.experimental.pallas import tpu as pltpu
from jax.sharding import PartitionSpec as P

TREMBLE = 0.05
AXES = ("trav", "bulk")

TRAV, BULK = 4, 8
X, Y, D, A, B, C = 1, 2, 3, 4, 12, 8
PLANE = (0, X, Y, D)
ID_ROWS = 16


def swap_chip(value, chip):
    return lax.ppermute(value, AXES, [(i, i ^ (chip << 1)) for i in range(TRAV * BULK)])


def swap_core(value):
    return lax.ppermute(value, AXES, [(i, i ^ 1) for i in range(TRAV * BULK)])


def iota(shape, dim):
    return lax.broadcasted_iota(jnp.int32, shape, dim)


def over_rows(a, b):
    return lax.dot_general(a, b, (((0,), (0,)), ((), ())), preferred_element_type=jnp.float32)


def my_core():
    return lax.axis_index("bulk") & 1


def my_chip():
    return lax.axis_index("trav") * (BULK // 2) + (lax.axis_index("bulk") >> 1)


def call(kernel, outs, mebibytes, scratch=()):
    many = isinstance(outs, (list, tuple))
    spec = pl.BlockSpec(memory_space=pltpu.VMEM)

    def run(*args):
        return pl.pallas_call(
            kernel,
            out_shape=tuple(outs) if many else outs,
            in_specs=[spec] * len(args),
            out_specs=(spec,) * len(outs) if many else spec,
            scratch_shapes=list(scratch),
            compiler_params=pltpu.CompilerParams(vmem_limit_bytes=mebibytes << 20),
        )(*args)

    return run


def shape(rows, columns, dtype=jnp.bfloat16):
    return jax.ShapeDtypeStruct((rows, columns), dtype)


def across(a, b, precision=None):
    return lax.dot_general(
        a, b, (((1,), (1,)), ((), ())), preferred_element_type=jnp.float32, precision=precision
    )


def keep_kernel(w_first, w_second, keep):
    one, half = w_first.shape[0], keep.shape[1]
    here = pl.ds(pl.multiple_of(my_core() * half, half), half)
    keep[:one, :] = w_first[:, here]
    keep[one:, :] = w_second[:, here]


def join_kernel(depths, keep, ids, other_first, other_second, other_owner, other_row, out, out_ids):
    core, half = my_core(), out.shape[1]
    here = pl.ds(pl.multiple_of(core * half, half), half)
    begin = 0
    for depth, other in zip(depths, (other_first, other_second)):
        for to, rows in ((core, keep[begin : begin + depth, :]), (1 - core, other[:, here])):
            place = pl.ds(pl.multiple_of(2 * begin + to * depth, depth), depth)
            for target in (out, out_ids):
                target[place, :] = rows
        begin += depth
    parts = [ref[...].astype(jnp.float32) for ref in (ids, other_owner, other_row)]
    count = ids.shape[1]
    parts = jnp.concatenate(parts + [jnp.zeros((ID_ROWS - 4, count), jnp.float32)], axis=0)
    parts = jnp.concatenate([parts, jnp.zeros((ID_ROWS, half - count), jnp.float32)], axis=1)
    out_ids[2 * begin :, :] = parts.astype(jnp.bfloat16)


def ranks_of(hits):
    count = hits.shape[1]
    before = (iota((count, count), 0) < iota((count, count), 1)).astype(jnp.bfloat16)
    return jnp.dot(hits.astype(jnp.bfloat16), before, preferred_element_type=jnp.float32)


def meta_kernel(capacity, owner, actions, out):
    partner = owner[...] ^ lax.axis_index("bulk")
    count = owner.shape[1]
    hits = (partner == iota((BULK, count), 0)).astype(jnp.float32)
    rank = jnp.sum(ranks_of(hits) * hits, axis=0, keepdims=True)
    slot = partner.astype(jnp.float32) * capacity + rank
    rows = out.shape[0]
    parts = [actions[...].astype(jnp.float32), slot, jnp.zeros((rows - actions.shape[0] - 1, count), jnp.float32)]
    parts = jnp.concatenate(parts, axis=0)
    out[...] = jnp.concatenate([parts, jnp.zeros((rows, out.shape[1] - count), jnp.float32)], axis=1).astype(jnp.bfloat16)


def serve_kernel(capacity, count, *refs):
    asked, table, outs = refs[: len(PLANE)], refs[len(PLANE)], refs[len(PLANE) + 1 :]
    buckets = table.shape[0]
    me = lax.axis_index("bulk")
    owners, rows = [], []
    for ids in asked:
        block = ids[ids.shape[0] - ID_ROWS :, :count].astype(jnp.float32)
        for core in (0, 1):
            owners.append(block[2 * core : 2 * core + 1, :])
            rows.append(block[2 * core + 1 : 2 * core + 2, :])
    owners, rows = jnp.concatenate(owners, axis=0), jnp.concatenate(rows, axis=0)
    hits = (owners.astype(jnp.int32) == me).astype(jnp.float32)
    ranks = ranks_of(hits).astype(jnp.int32)
    rows = (rows * hits).astype(jnp.bfloat16)
    wants = []
    for j in range(2 * len(PLANE)):
        at_rank = (ranks[j : j + 1, :] == iota((capacity, count), 0)).astype(jnp.bfloat16)
        wants.append(across(rows, at_rank)[j : j + 1, :])
    want = jnp.concatenate(wants, axis=1).astype(jnp.int32)
    onehot = (iota((buckets, want.shape[1]), 0) == want).astype(jnp.bfloat16)
    found = over_rows(onehot, table[...]).astype(jnp.bfloat16)
    for n, out in enumerate(outs):
        out[...] = found[2 * n * capacity : 2 * (n + 1) * capacity, :]


def inputs_kernel(capacity, branch_slots, act_table, mine, theirs, out):
    served = len(PLANE) * 2 * capacity
    rows = out.shape[0] // (2 * branch_slots)
    to = 0
    for which, ref in enumerate((mine, theirs)):
        parts = []
        for n in range(len(PLANE)):
            for core in (0, 1):
                begin = (2 * n + core) * capacity
                parts.append((mine, theirs)[which ^ core][begin : begin + capacity, :])
        buckets = jnp.concatenate(parts, axis=0)
        meta = ref[served + rows :, :rows].astype(jnp.float32).astype(jnp.int32)
        onehot = (meta[branch_slots : branch_slots + 1, :] == iota((served, rows), 0)).astype(jnp.bfloat16)
        bucket = over_rows(onehot, buckets)
        parent = ref[served : served + rows, :].astype(jnp.float32)
        acts = jnp.concatenate([meta[c : c + 1, :] for c in range(branch_slots)], axis=1)
        onehot = (acts == iota((act_table.shape[0], branch_slots * rows), 0)).astype(jnp.bfloat16)
        change = over_rows(onehot, act_table[...])
        for c in range(branch_slots):
            base = (parent + change[c * rows : (c + 1) * rows, :]).astype(jnp.bfloat16)
            out[to : to + rows, :] = (base.astype(jnp.float32) + bucket).astype(jnp.bfloat16)
            to += rows


def place_kernel(pieces, depth, *refs):
    refs, out = refs[:-1], refs[-1]
    for chip, which, begin, row, count in pieces:
        to = pl.multiple_of((my_chip() ^ chip) * depth + row, 16)
        out[pl.ds(to, count), :] = refs[which][begin : begin + count, :]


def first_kernel(depth, inputs, home, other, bias, out):
    half = home.shape[1]
    chips = half // depth
    me, core = my_chip(), my_core()
    rows, group = inputs.shape[0] // 2, 4
    for which, weights in enumerate((home, other)):
        side = core ^ which
        base = ((me // chips) ^ side) * half
        for first in range(0, chips, group):
            spots = [(n ^ me) & (chips - 1) for n in range(first, first + group)]
            columns = [pl.ds(pl.multiple_of(spot * depth, depth), depth) for spot in spots]
            shifts = [pl.ds(pl.multiple_of(side * half + spot * depth, depth), depth) for spot in spots]
            block = jnp.concatenate([weights[:, column] for column in columns], axis=1)
            shift = jnp.concatenate([bias[:, column] for column in shifts], axis=1)
            to = pl.ds(pl.multiple_of(base + first * depth, group * depth), group * depth)
            for m in (0, rows):
                total = jnp.dot(inputs[m : m + rows, :], block, preferred_element_type=jnp.float32)
                out[m : m + rows, to] = jnp.maximum(total + shift, 0.0).astype(jnp.bfloat16)


def line_up(pieces, refs, depth, weights):
    order = list(dict.fromkeys(piece[0] for piece in pieces))
    for name, which, begin, row, count in pieces:
        to = order.index(name) * depth + row
        weights[to : to + count, :] = refs[which][begin : begin + count, :]
    return [slice(name * depth, (name + 1) * depth) for name in order]


def second_kernel(pieces, depth, hidden, *refs):
    refs, (out, weights) = refs[:-2], refs[-2:]
    columns = line_up(pieces, refs, depth, weights)
    step, rows = 512, hidden.shape[0] // 2
    for m in (0, rows):
        picked = jnp.concatenate([hidden[m : m + rows, column] for column in columns], axis=1)
        for n in range(0, out.shape[1], step):
            out[m : m + rows, n : n + step] = jnp.dot(
                picked, weights[:, n : n + step], preferred_element_type=jnp.float32
            )


def finish_second(names, depth, first, hidden, so_far, bias, w_head, weights, out):
    half, core, rows = so_far.shape[1], my_core(), out.shape[1]
    here = slice(first, first + rows)
    picked = jnp.concatenate([hidden[here, name * depth : (name + 1) * depth] for name in names], axis=1)
    advantage = jnp.zeros((rows, w_head.shape[0]), jnp.float32)
    step = 512
    for n in range(0, half, step):
        columns = pl.ds(pl.multiple_of(core * half + n, step), step)
        total = so_far[here, n : n + step] + jnp.dot(
            picked, weights[:, n : n + step], preferred_element_type=jnp.float32
        )
        layer = jnp.maximum(total + bias[:, columns], 0.0).astype(jnp.bfloat16)
        advantage = advantage + across(layer, w_head[:, columns])
    out[...] = advantage.T


def theirs_kernel(pieces, names, depth, first, hidden, so_far, bias, w_head, *refs):
    refs, (out, weights) = refs[:-2], refs[-2:]
    line_up(pieces, refs, depth, weights)
    finish_second(names, depth, first, hidden, so_far, bias, w_head, weights, out)


def stack_kernel(places, *refs):
    refs, out = refs[:-1], refs[-1]
    to = 0
    for ref, (begin, count) in zip(refs, places):
        out[to : to + count, :] = ref[begin : begin + count, :]
        to += count


def stack(*parts):
    arrays, places = [part[0] for part in parts], [part[1:] for part in parts]
    total = sum(count for _, count in places)
    out = shape(total, arrays[0].shape[1], arrays[0].dtype)
    return call(functools.partial(stack_kernel, places), out, 4)(*arrays)


def last_kernel(counts, ancestor, legal, b_head, mine, theirs, strategy, values):
    actions = b_head.shape[1]
    rows = counts.shape[1]
    diagonal = iota((actions, actions), 0) == iota((actions, actions), 1)
    shift = jnp.sum(jnp.where(diagonal, b_head[...], 0.0), axis=1, keepdims=True)
    first_action = (iota((actions, rows), 0) == 0).astype(jnp.float32)
    total_value = jnp.zeros((1, rows), jnp.float32)
    for c in range(mine.shape[1] // rows):
        here = slice(c * rows, (c + 1) * rows)
        advantage = mine[:, here] + theirs[:, here] + shift
        allowed = jnp.maximum(legal[c * actions : (c + 1) * actions, :].astype(jnp.float32), first_action)
        positive = allowed * (jnp.maximum(advantage, 0.0) + TREMBLE)
        sigma = positive / jnp.sum(positive, axis=0, keepdims=True)
        live = (counts[...] > c).astype(jnp.float32)
        strategy[c * actions : (c + 1) * actions, :] = sigma * live
        total_value = total_value + live * jnp.sum(sigma * advantage, axis=0, keepdims=True)
    value = total_value / counts[...].astype(jnp.float32)
    at_node = (ancestor[...] == iota((values.shape[1], rows), 0)).astype(jnp.float32)
    values[...] = across(value, at_node, lax.Precision.HIGHEST)


def body(
    parents,
    act_table,
    bucket_table,
    w_first,
    b_first,
    w_second,
    b_second,
    w_head,
    b_head,
    branch_counts,
    sampled_actions,
    bucket_owner,
    bucket_row,
    legal_mask,
    ancestor,
):
    par_count, feature_count = parents.shape
    branch_slots = sampled_actions.shape[1]
    branches = par_count * branch_slots
    hidden_units = w_first.shape[1]
    half = hidden_units // 2
    depth_one, depth_two = w_first.shape[0], w_second.shape[0]
    chip_one, chip_two = 2 * depth_one, 2 * depth_two
    depth = chip_one + chip_two
    capacity = max(2, (4 * par_count + 3 * BULK - 1) // (3 * BULK))
    wide = 2 * capacity

    owner, row = bucket_owner.T, bucket_row[None, :]
    keep = call(keep_kernel, shape(depth // 2, half), 4)(w_first, w_second)
    ids = jnp.concatenate([owner, row], axis=0)
    own, own_ids = call(
        functools.partial(join_kernel, (depth_one, depth_two)), (shape(depth, half), shape(depth + ID_ROWS, half)), 4
    )(keep, ids, swap_core(w_first), swap_core(w_second), swap_core(owner), swap_core(row))
    from_x, from_y, from_d = [swap_chip(own_ids, chip) for chip in PLANE[1:]]
    from_a, from_b = [swap_chip(own, chip) for chip in (A, B)]
    meta = call(functools.partial(meta_kernel, capacity), shape(ID_ROWS, feature_count), 4)(owner, sampled_actions.T)
    table = stack((bucket_table, 0, bucket_table.shape[0]))
    from_x, from_y, from_d, from_a, table = lax.optimization_barrier((from_x, from_y, from_d, from_a, table))

    served = call(
        functools.partial(serve_kernel, capacity, par_count), (shape(wide, feature_count),) * len(PLANE), 6
    )(own_ids, from_x, from_y, from_d, table)
    few = chip_one // 2
    x_ab = swap_chip(stack((from_a, few, depth - few), (from_b, 0, depth), (served[1], 0, wide)), X)
    y_ab = swap_chip(stack((from_a, few, depth - few), (from_b, 0, depth), (served[2], 0, wide)), Y)
    rows_d = swap_chip(stack((served[3], 0, wide), (from_b, 0, chip_one)), D)
    c_da = swap_chip(stack((from_b, 0, depth), (from_d, 0, chip_one), (from_x, 0, few), (from_y, 0, few)), A)
    plane_c = swap_chip(stack((from_x, 0, chip_one), (from_y, 0, chip_one), (from_d, 0, chip_one)), C)
    x_ab, y_ab, rows_d, c_da, plane_c = lax.optimization_barrier((x_ab, y_ab, rows_d, c_da, plane_c))

    cut = chip_two // 2
    at_a, at_b = chip_one - few, depth - few + chip_one
    x_c = swap_chip(stack((c_da, chip_one, chip_two), (y_ab, at_a, cut), (y_ab, at_b, cut)), X)
    y_c = swap_chip(stack((c_da, chip_one, chip_two), (x_ab, at_a + cut, cut), (x_ab, at_b + cut, cut)), Y)
    d_c = swap_chip(stack((from_d, chip_one, chip_two)), C)

    end = 2 * depth - few
    mine = stack(
        (served[0], 0, wide), (x_ab, end, wide), (y_ab, end, wide), (rows_d, 0, wide),
        (parents, 0, par_count), (meta, 0, ID_ROWS)
    )
    inputs = call(functools.partial(inputs_kernel, capacity, branch_slots), shape(2 * branches, feature_count), 10)(
        act_table, mine, swap_core(mine)
    )

    arrays = [own, from_x, from_y, from_a, from_b, from_d, x_ab, y_ab, c_da]
    near = [(chip, n) for n, chip in enumerate((0, X, Y, A, B, D))]
    first_pieces = [(chip, n, 0, 0, chip_one) for chip, n in near] + [(C, 8, 0, 0, chip_one)]
    for n, chip in ((6, X), (7, Y)):
        first_pieces.append((chip ^ A, 8, depth + chip_one + (n - 6) * few, 0, few))
        first_pieces += [(chip ^ A, n, 0, few, chip_one - few), (chip ^ B, n, depth - few, 0, chip_one)]
    first_pieces += [(D ^ A, 8, depth, 0, chip_one), (D ^ B, 9, wide, 0, chip_one)]
    first_pieces += [(chip ^ C, 10, n * chip_one, 0, chip_one) for n, chip in enumerate((X, Y, D))]
    weights = call(functools.partial(place_kernel, first_pieces, chip_one), shape(feature_count, half), 4)(
        *arrays, rows_d, plane_c
    )
    hidden = call(functools.partial(first_kernel, chip_two), shape(2 * branches, hidden_units), 12)(
        inputs, weights, swap_core(weights), b_first[None, :]
    )

    early = [(chip, n, chip_one, 0, chip_two) for chip, n in near]
    for n, chip in ((6, X), (7, Y)):
        early += [(chip ^ A, n, at_a, 0, chip_two), (chip ^ B, n, at_b, 0, chip_two)]
    early.sort()
    so_far = call(
        functools.partial(second_kernel, early, chip_two),
        shape(2 * branches, half, jnp.float32),
        16,
        [pltpu.VMEM((len({piece[0] for piece in early}) * chip_two, half), jnp.bfloat16)],
    )(hidden, *arrays)
    late = [(C, 3, chip_one, 0, chip_two), (X ^ C, 0, 0, 0, chip_two), (Y ^ C, 1, 0, 0, chip_two)]
    late += [(D ^ C, 2, 0, 0, chip_two)]
    late += [(D ^ A, 0, chip_two, 0, cut), (D ^ A, 1, chip_two, cut, cut)]
    late += [(D ^ B, 0, chip_two + cut, 0, cut), (D ^ B, 1, chip_two + cut, cut, cut)]
    names = list(dict.fromkeys(piece[0] for piece in late))
    partial = shape(w_head.shape[1], branches, jnp.float32)
    common = (hidden, so_far, b_second[None, :], w_head.T)
    theirs, late_weights = call(
        functools.partial(theirs_kernel, late, names, chip_two, branches),
        (partial, shape(len(names) * chip_two, half)),
        12,
    )(*common, x_c, y_c, d_c, c_da)
    mine = call(functools.partial(finish_second, names, chip_two, 0), partial, 10)(*common, late_weights)
    strategy, values = call(
        last_kernel, (shape(legal_mask.shape[1], par_count, jnp.float32), shape(1, par_count // 4, jnp.float32)), 4
    )(branch_counts[None, :], ancestor[None, :], legal_mask.T, b_head[None, :], mine, swap_core(theirs))
    return (strategy.T, values.reshape(-1))


def network(inputs, w_first, b_first, w_second, b_second, w_head, b_head):
    columns = inputs
    first = jnp.dot(
        columns,
        lax.all_gather(w_first, ("trav", "bulk"), axis=0, tiled=True),
        preferred_element_type=jnp.float32,
    )
    hidden_one = jnp.maximum(first + b_first, 0.0).astype(jnp.bfloat16)
    columns = hidden_one
    second = jnp.dot(
        columns,
        lax.all_gather(w_second, ("trav", "bulk"), axis=0, tiled=True),
        preferred_element_type=jnp.float32,
    )
    hidden_two = jnp.maximum(second + b_second, 0.0).astype(jnp.bfloat16)
    return jnp.dot(hidden_two, w_head, preferred_element_type=jnp.float32) + b_head


def general_body(
    parents,
    act_table,
    bucket_table,
    w_first,
    b_first,
    w_second,
    b_second,
    w_head,
    b_head,
    branch_counts,
    sampled_actions,
    bucket_owner,
    bucket_row,
    legal_mask,
    ancestor,
):
    par_count = parents.shape[0]
    feature_count = parents.shape[1]
    branch_slots = sampled_actions.shape[1]
    vocab_size = act_table.shape[0]
    action_count = w_head.shape[1]
    bulk_count = lax.axis_size("bulk")
    capacity = max(2, (4 * par_count + 3 * bulk_count - 1) // (3 * bulk_count))
    slot_total = bulk_count * capacity
    action_onehot = (
        sampled_actions.reshape(-1)[:, None] == jnp.arange(vocab_size)[None, :]
    ).astype(jnp.bfloat16)
    act_rows = jnp.dot(action_onehot, act_table, preferred_element_type=jnp.float32)
    base = (jnp.repeat(parents.astype(jnp.float32), branch_slots, axis=0) + act_rows).astype(
        jnp.bfloat16
    )
    base = lax.optimization_barrier(base)
    owner_index = bucket_owner[:, 0]
    owner_hits = (owner_index[:, None] == jnp.arange(bulk_count)[None, :]).astype(jnp.int32)
    earlier = jnp.cumsum(owner_hits, axis=0) - owner_hits
    slot_index = owner_index * capacity + jnp.sum(earlier * owner_hits, axis=1)
    placement_int = (slot_index[None, :] == jnp.arange(slot_total)[:, None]).astype(jnp.int32)
    slot_bucket = jnp.sum(placement_int * bucket_row[None, :], axis=1).reshape(bulk_count, capacity)
    placement = placement_int.astype(jnp.bfloat16)
    outgoing = jnp.dot(
        placement,
        base.reshape(par_count, branch_slots * feature_count),
        preferred_element_type=jnp.float32,
    )
    outgoing = outgoing.astype(jnp.bfloat16).reshape(
        bulk_count, capacity * branch_slots, feature_count
    )
    arrived_rows = lax.all_to_all(outgoing, "bulk", split_axis=0, concat_axis=0, tiled=True)
    arrived_ids = lax.all_to_all(slot_bucket, "bulk", split_axis=0, concat_axis=0, tiled=True)
    table_rows = jnp.take(bucket_table, arrived_ids.reshape(-1), axis=0)
    inputs = (
        arrived_rows.reshape(slot_total, branch_slots, feature_count).astype(jnp.float32)
        + table_rows.astype(jnp.float32)[:, None, :]
    )
    inputs = inputs.astype(jnp.bfloat16).reshape(slot_total * branch_slots, feature_count)
    evaluated = network(inputs, w_first, b_first, w_second, b_second, w_head, b_head)
    returned = lax.all_to_all(
        evaluated.reshape(bulk_count, capacity * branch_slots * action_count).astype(jnp.bfloat16),
        "bulk",
        split_axis=0,
        concat_axis=0,
        tiled=True,
    ).astype(jnp.float32)
    advantage = jnp.take(
        returned.reshape(slot_total, branch_slots * action_count), slot_index, axis=0
    )
    advantage = advantage.reshape(par_count, branch_slots, action_count)
    first_action = (jnp.arange(action_count) == 0).astype(jnp.float32)
    allowed = jnp.maximum(
        legal_mask.reshape(par_count, branch_slots, action_count).astype(jnp.float32), first_action
    )
    positive = allowed * (jnp.maximum(advantage, 0.0) + TREMBLE)
    sigma = positive / jnp.sum(positive, axis=-1, keepdims=True)
    live = (jnp.arange(branch_slots)[None, :] < branch_counts[:, None]).astype(jnp.float32)
    strategy = (sigma * live[:, :, None]).reshape(par_count, branch_slots * action_count)
    branch_value = jnp.sum(sigma * advantage, axis=-1)
    history_value = jnp.sum(branch_value * live, axis=1) / branch_counts.astype(jnp.float32)
    node_count = par_count // 4
    node_onehot = (ancestor[:, None] == jnp.arange(node_count)[None, :]).astype(jnp.float32)
    ancestor_value = jnp.sum(node_onehot * history_value[:, None], axis=0)
    return (strategy, ancestor_value)


def solution(mesh):
    laid_out = (mesh.shape["trav"], mesh.shape["bulk"]) == (TRAV, BULK)
    return jax.shard_map(
        body if laid_out else general_body,
        mesh=mesh,
        in_specs=(
            P(AXES, None),
            P(),
            P("bulk", None),
            P(AXES, None),
            P(),
            P(AXES, None),
            P(),
            P(),
            P(),
            P(AXES),
            P(AXES, None),
            P(AXES, None),
            P(AXES),
            P(AXES, None),
            P(AXES),
        ),
        out_specs=(P(AXES, None), P(AXES)),
        check_vma=False,
    )
```

```python
import functools

import jax
import jax.numpy as jnp
from jax import lax
from jax.experimental import pallas as pl
from jax.experimental.pallas import tpu as pltpu
from jax.sharding import PartitionSpec as P

TREMBLE = 0.05
AXES = ("trav", "bulk")

TRAV, BULK = 4, 8
X, Y, D, A, B, C = 1, 2, 3, 4, 12, 8
PLANE = (0, X, Y, D)
ID_ROWS = 16


def swap_chip(value, chip):
    return lax.ppermute(value, AXES, [(i, i ^ (chip << 1)) for i in range(TRAV * BULK)])


def swap_core(value):
    return lax.ppermute(value, AXES, [(i, i ^ 1) for i in range(TRAV * BULK)])


def iota(shape, dim):
    return lax.broadcasted_iota(jnp.int32, shape, dim)


def over_rows(a, b):
    return lax.dot_general(a, b, (((0,), (0,)), ((), ())), preferred_element_type=jnp.float32)


def my_core():
    return lax.axis_index("bulk") & 1


def my_chip():
    return lax.axis_index("trav") * (BULK // 2) + (lax.axis_index("bulk") >> 1)


def call(kernel, outs, mebibytes, scratch=()):
    many = isinstance(outs, (list, tuple))
    spec = pl.BlockSpec(memory_space=pltpu.VMEM)

    def run(*args):
        return pl.pallas_call(
            kernel,
            out_shape=tuple(outs) if many else outs,
            in_specs=[spec] * len(args),
            out_specs=(spec,) * len(outs) if many else spec,
            scratch_shapes=list(scratch),
            compiler_params=pltpu.CompilerParams(vmem_limit_bytes=mebibytes << 20),
        )(*args)

    return run


def shape(rows, columns, dtype=jnp.bfloat16):
    return jax.ShapeDtypeStruct((rows, columns), dtype)


def across(a, b, precision=None):
    return lax.dot_general(
        a, b, (((1,), (1,)), ((), ())), preferred_element_type=jnp.float32, precision=precision
    )


def keep_kernel(w_first, w_second, keep):
    one, half = w_first.shape[0], keep.shape[1]
    here = pl.ds(pl.multiple_of(my_core() * half, half), half)
    keep[:one, :] = w_first[:, here]
    keep[one:, :] = w_second[:, here]


def join_kernel(depths, keep, ids, other_first, other_second, other_owner, other_row, out, out_ids):
    core, half = my_core(), out.shape[1]
    here = pl.ds(pl.multiple_of(core * half, half), half)
    begin = 0
    for depth, other in zip(depths, (other_first, other_second)):
        for to, rows in ((core, keep[begin : begin + depth, :]), (1 - core, other[:, here])):
            place = pl.ds(pl.multiple_of(2 * begin + to * depth, depth), depth)
            for target in (out, out_ids):
                target[place, :] = rows
        begin += depth
    parts = [ref[...].astype(jnp.float32) for ref in (ids, other_owner, other_row)]
    count = ids.shape[1]
    parts = jnp.concatenate(parts + [jnp.zeros((ID_ROWS - 4, count), jnp.float32)], axis=0)
    parts = jnp.concatenate([parts, jnp.zeros((ID_ROWS, half - count), jnp.float32)], axis=1)
    out_ids[2 * begin :, :] = parts.astype(jnp.bfloat16)


def ranks_of(hits):
    count = hits.shape[1]
    before = (iota((count, count), 0) < iota((count, count), 1)).astype(jnp.bfloat16)
    return jnp.dot(hits.astype(jnp.bfloat16), before, preferred_element_type=jnp.float32)


def meta_kernel(capacity, owner, actions, out):
    partner = owner[...] ^ lax.axis_index("bulk")
    count = owner.shape[1]
    hits = (partner == iota((BULK, count), 0)).astype(jnp.float32)
    rank = jnp.sum(ranks_of(hits) * hits, axis=0, keepdims=True)
    slot = partner.astype(jnp.float32) * capacity + rank
    rows = out.shape[0]
    parts = [actions[...].astype(jnp.float32), slot, jnp.zeros((rows - actions.shape[0] - 1, count), jnp.float32)]
    parts = jnp.concatenate(parts, axis=0)
    out[...] = jnp.concatenate([parts, jnp.zeros((rows, out.shape[1] - count), jnp.float32)], axis=1).astype(jnp.bfloat16)


def serve_kernel(capacity, count, *refs):
    asked, table, outs = refs[: len(PLANE)], refs[len(PLANE)], refs[len(PLANE) + 1 :]
    buckets = table.shape[0]
    me = lax.axis_index("bulk")
    owners, rows = [], []
    for ids in asked:
        block = ids[ids.shape[0] - ID_ROWS :, :count].astype(jnp.float32)
        for core in (0, 1):
            owners.append(block[2 * core : 2 * core + 1, :])
            rows.append(block[2 * core + 1 : 2 * core + 2, :])
    owners, rows = jnp.concatenate(owners, axis=0), jnp.concatenate(rows, axis=0)
    hits = (owners.astype(jnp.int32) == me).astype(jnp.float32)
    ranks = ranks_of(hits).astype(jnp.int32)
    rows = (rows * hits).astype(jnp.bfloat16)
    wants = []
    for j in range(2 * len(PLANE)):
        at_rank = (ranks[j : j + 1, :] == iota((capacity, count), 0)).astype(jnp.bfloat16)
        wants.append(across(rows, at_rank)[j : j + 1, :])
    want = jnp.concatenate(wants, axis=1).astype(jnp.int32)
    onehot = (iota((buckets, want.shape[1]), 0) == want).astype(jnp.bfloat16)
    found = over_rows(onehot, table[...]).astype(jnp.bfloat16)
    for n, out in enumerate(outs):
        out[...] = found[2 * n * capacity : 2 * (n + 1) * capacity, :]


def inputs_kernel(capacity, branch_slots, act_table, mine, theirs, out):
    served = len(PLANE) * 2 * capacity
    rows = out.shape[0] // (2 * branch_slots)
    to = 0
    for which, ref in enumerate((mine, theirs)):
        parts = []
        for n in range(len(PLANE)):
            for core in (0, 1):
                begin = (2 * n + core) * capacity
                parts.append((mine, theirs)[which ^ core][begin : begin + capacity, :])
        buckets = jnp.concatenate(parts, axis=0)
        meta = ref[served + rows :, :rows].astype(jnp.float32).astype(jnp.int32)
        onehot = (meta[branch_slots : branch_slots + 1, :] == iota((served, rows), 0)).astype(jnp.bfloat16)
        bucket = over_rows(onehot, buckets)
        parent = ref[served : served + rows, :].astype(jnp.float32)
        acts = jnp.concatenate([meta[c : c + 1, :] for c in range(branch_slots)], axis=1)
        onehot = (acts == iota((act_table.shape[0], branch_slots * rows), 0)).astype(jnp.bfloat16)
        change = over_rows(onehot, act_table[...])
        for c in range(branch_slots):
            base = (parent + change[c * rows : (c + 1) * rows, :]).astype(jnp.bfloat16)
            out[to : to + rows, :] = (base.astype(jnp.float32) + bucket).astype(jnp.bfloat16)
            to += rows


def place_kernel(pieces, depth, *refs):
    refs, out = refs[:-1], refs[-1]
    for chip, which, begin, row, count in pieces:
        to = pl.multiple_of((my_chip() ^ chip) * depth + row, 16)
        out[pl.ds(to, count), :] = refs[which][begin : begin + count, :]


def first_kernel(depth, inputs, home, other, bias, out):
    half = home.shape[1]
    chips = half // depth
    me, core = my_chip(), my_core()
    rows, group = inputs.shape[0] // 2, 4
    for which, weights in enumerate((home, other)):
        side = core ^ which
        base = ((me // chips) ^ side) * half
        for first in range(0, chips, group):
            spots = [(n ^ me) & (chips - 1) for n in range(first, first + group)]
            columns = [pl.ds(pl.multiple_of(spot * depth, depth), depth) for spot in spots]
            shifts = [pl.ds(pl.multiple_of(side * half + spot * depth, depth), depth) for spot in spots]
            block = jnp.concatenate([weights[:, column] for column in columns], axis=1)
            shift = jnp.concatenate([bias[:, column] for column in shifts], axis=1)
            to = pl.ds(pl.multiple_of(base + first * depth, group * depth), group * depth)
            for m in (0, rows):
                total = jnp.dot(inputs[m : m + rows, :], block, preferred_element_type=jnp.float32)
                out[m : m + rows, to] = jnp.maximum(total + shift, 0.0).astype(jnp.bfloat16)


def line_up(pieces, refs, depth, weights):
    order = list(dict.fromkeys(piece[0] for piece in pieces))
    for name, which, begin, row, count in pieces:
        to = order.index(name) * depth + row
        weights[to : to + count, :] = refs[which][begin : begin + count, :]
    return [slice(name * depth, (name + 1) * depth) for name in order]


def second_kernel(pieces, depth, hidden, *refs):
    refs, (out, weights) = refs[:-2], refs[-2:]
    columns = line_up(pieces, refs, depth, weights)
    step, rows = 512, hidden.shape[0] // 2
    for m in (0, rows):
        picked = jnp.concatenate([hidden[m : m + rows, column] for column in columns], axis=1)
        for n in range(0, out.shape[1], step):
            out[m : m + rows, n : n + step] = jnp.dot(
                picked, weights[:, n : n + step], preferred_element_type=jnp.float32
            )


def finish_second(names, depth, first, hidden, so_far, bias, w_head, weights, out):
    half, core, rows = so_far.shape[1], my_core(), out.shape[1]
    here = slice(first, first + rows)
    picked = jnp.concatenate([hidden[here, name * depth : (name + 1) * depth] for name in names], axis=1)
    advantage = jnp.zeros((rows, w_head.shape[0]), jnp.float32)
    step = 512
    for n in range(0, half, step):
        columns = pl.ds(pl.multiple_of(core * half + n, step), step)
        total = so_far[here, n : n + step] + jnp.dot(
            picked, weights[:, n : n + step], preferred_element_type=jnp.float32
        )
        layer = jnp.maximum(total + bias[:, columns], 0.0).astype(jnp.bfloat16)
        advantage = advantage + across(layer, w_head[:, columns])
    out[...] = advantage.T


def theirs_kernel(pieces, names, depth, first, hidden, so_far, bias, w_head, *refs):
    refs, (out, weights) = refs[:-2], refs[-2:]
    line_up(pieces, refs, depth, weights)
    finish_second(names, depth, first, hidden, so_far, bias, w_head, weights, out)


def stack_kernel(places, *refs):
    refs, out = refs[:-1], refs[-1]
    to = 0
    for ref, (begin, count) in zip(refs, places):
        out[to : to + count, :] = ref[begin : begin + count, :]
        to += count


def stack(*parts):
    arrays, places = [part[0] for part in parts], [part[1:] for part in parts]
    total = sum(count for _, count in places)
    out = shape(total, arrays[0].shape[1], arrays[0].dtype)
    return call(functools.partial(stack_kernel, places), out, 4)(*arrays)


def last_kernel(counts, ancestor, legal, b_head, mine, theirs, strategy, values):
    actions = b_head.shape[1]
    rows = counts.shape[1]
    diagonal = iota((actions, actions), 0) == iota((actions, actions), 1)
    shift = jnp.sum(jnp.where(diagonal, b_head[...], 0.0), axis=1, keepdims=True)
    first_action = (iota((actions, rows), 0) == 0).astype(jnp.float32)
    total_value = jnp.zeros((1, rows), jnp.float32)
    for c in range(mine.shape[1] // rows):
        here = slice(c * rows, (c + 1) * rows)
        advantage = mine[:, here] + theirs[:, here] + shift
        allowed = jnp.maximum(legal[c * actions : (c + 1) * actions, :].astype(jnp.float32), first_action)
        positive = allowed * (jnp.maximum(advantage, 0.0) + TREMBLE)
        sigma = positive / jnp.sum(positive, axis=0, keepdims=True)
        live = (counts[...] > c).astype(jnp.float32)
        strategy[c * actions : (c + 1) * actions, :] = sigma * live
        total_value = total_value + live * jnp.sum(sigma * advantage, axis=0, keepdims=True)
    value = total_value / counts[...].astype(jnp.float32)
    at_node = (ancestor[...] == iota((values.shape[1], rows), 0)).astype(jnp.float32)
    values[...] = across(value, at_node, lax.Precision.HIGHEST)


def body(
    parents,
    act_table,
    bucket_table,
    w_first,
    b_first,
    w_second,
    b_second,
    w_head,
    b_head,
    branch_counts,
    sampled_actions,
    bucket_owner,
    bucket_row,
    legal_mask,
    ancestor,
):
    par_count, feature_count = parents.shape
    branch_slots = sampled_actions.shape[1]
    branches = par_count * branch_slots
    hidden_units = w_first.shape[1]
    half = hidden_units // 2
    depth_one, depth_two = w_first.shape[0], w_second.shape[0]
    chip_one, chip_two = 2 * depth_one, 2 * depth_two
    depth = chip_one + chip_two
    capacity = max(2, (4 * par_count + 3 * BULK - 1) // (3 * BULK))
    wide = 2 * capacity

    owner, row = bucket_owner.T, bucket_row[None, :]
    keep = call(keep_kernel, shape(depth // 2, half), 4)(w_first, w_second)
    ids = jnp.concatenate([owner, row], axis=0)
    own, own_ids = call(
        functools.partial(join_kernel, (depth_one, depth_two)), (shape(depth, half), shape(depth + ID_ROWS, half)), 4
    )(keep, ids, swap_core(w_first), swap_core(w_second), swap_core(owner), swap_core(row))
    from_x, from_y, from_d = [swap_chip(own_ids, chip) for chip in PLANE[1:]]
    from_a, from_b = [swap_chip(own, chip) for chip in (A, B)]
    meta = call(functools.partial(meta_kernel, capacity), shape(ID_ROWS, feature_count), 4)(owner, sampled_actions.T)
    table = stack((bucket_table, 0, bucket_table.shape[0]))
    from_x, from_y, from_d, from_a, table = lax.optimization_barrier((from_x, from_y, from_d, from_a, table))

    served = call(
        functools.partial(serve_kernel, capacity, par_count), (shape(wide, feature_count),) * len(PLANE), 6
    )(own_ids, from_x, from_y, from_d, table)
    some = chip_one // 4
    few, rest = chip_one // 4, 3 * chip_two // 8
    x_ab = swap_chip(
        stack(
            (from_a, few, depth - few), (from_b, 0, chip_one), (from_b, chip_one + rest, chip_two - rest),
            (served[1], 0, wide)
        ),
        X,
    )
    y_ab = swap_chip(stack((from_a, few, depth - few), (from_b, 0, depth - rest), (served[2], 0, wide)), Y)
    rows_d = swap_chip(stack((served[3], 0, wide), (from_b, 0, chip_one)), D)
    c_da = swap_chip(stack((from_b, 0, depth), (from_d, 0, chip_one), (from_x, 0, few), (from_y, 0, few)), A)
    plane_c = swap_chip(stack((from_x, 0, chip_one), (from_y, 0, chip_one), (from_d, 0, chip_one + some)), C)
    x_ab, y_ab, rows_d, c_da, plane_c = lax.optimization_barrier((x_ab, y_ab, rows_d, c_da, plane_c))

    cut = chip_two // 2
    at_a, at_b = chip_one - few, depth - few + chip_one
    x_c = swap_chip(
        stack((c_da, chip_one, chip_two), (y_ab, at_a, cut), (y_ab, at_b, cut), (from_b, chip_one, rest)), X
    )
    y_c = swap_chip(
        stack(
            (c_da, chip_one, chip_two), (x_ab, at_a + cut, cut), (x_ab, at_b + cut - rest, cut),
            (from_b, depth - rest, rest)
        ),
        Y,
    )
    d_c = swap_chip(stack((from_d, chip_one + some, chip_two - some)), C)

    end = 2 * depth - few - rest
    mine = stack(
        (served[0], 0, wide), (x_ab, end, wide), (y_ab, end, wide), (rows_d, 0, wide),
        (parents, 0, par_count), (meta, 0, ID_ROWS)
    )
    inputs = call(functools.partial(inputs_kernel, capacity, branch_slots), shape(2 * branches, feature_count), 10)(
        act_table, mine, swap_core(mine)
    )

    arrays = [own, from_x, from_y, from_a, from_b, from_d, x_ab, y_ab, c_da]
    near = [(chip, n) for n, chip in enumerate((0, X, Y, A, B, D))]
    first_pieces = [(chip, n, 0, 0, chip_one) for chip, n in near] + [(C, 8, 0, 0, chip_one)]
    for n, chip in ((6, X), (7, Y)):
        first_pieces.append((chip ^ A, 8, depth + chip_one + (n - 6) * few, 0, few))
        first_pieces += [(chip ^ A, n, 0, few, chip_one - few), (chip ^ B, n, depth - few, 0, chip_one)]
    first_pieces += [(D ^ A, 8, depth, 0, chip_one), (D ^ B, 9, wide, 0, chip_one)]
    first_pieces += [(chip ^ C, 10, n * chip_one, 0, chip_one) for n, chip in enumerate((X, Y, D))]
    weights = call(functools.partial(place_kernel, first_pieces, chip_one), shape(feature_count, half), 4)(
        *arrays, rows_d, plane_c
    )
    hidden = call(functools.partial(first_kernel, chip_two), shape(2 * branches, hidden_units), 12)(
        inputs, weights, swap_core(weights), b_first[None, :]
    )

    early = [(chip, n, chip_one, 0, chip_two) for chip, n in near]
    for n, chip in ((6, X), (7, Y)):
        early.append((chip ^ A, n, at_a, 0, chip_two))
    early.sort()
    so_far = call(
        functools.partial(second_kernel, early, chip_two),
        shape(2 * branches, half, jnp.float32),
        16,
        [pltpu.VMEM((len({piece[0] for piece in early}) * chip_two, half), jnp.bfloat16)],
    )(hidden, *arrays)
    late = [(C, 3, chip_one, 0, chip_two), (X ^ C, 0, 0, 0, chip_two), (Y ^ C, 1, 0, 0, chip_two)]
    late += [(D ^ C, 6, 3 * chip_one, 0, some), (D ^ C, 2, 0, some, chip_two - some)]
    late += [(D ^ A, 0, chip_two, 0, cut), (D ^ A, 1, chip_two, cut, cut)]
    late += [(D ^ B, 0, chip_two + cut, 0, cut), (D ^ B, 1, chip_two + cut, cut, cut)]
    tail = chip_two + 2 * cut
    late += [(X ^ B, 4, at_b, rest, chip_two - rest), (X ^ B, 0, tail, 0, rest)]
    late += [(Y ^ B, 5, at_b, 0, chip_two - rest), (Y ^ B, 1, tail, chip_two - rest, rest)]
    names = list(dict.fromkeys(piece[0] for piece in late))
    partial = shape(w_head.shape[1], branches, jnp.float32)
    common = (hidden, so_far, b_second[None, :], w_head.T)
    theirs, late_weights = call(
        functools.partial(theirs_kernel, late, names, chip_two, branches),
        (partial, shape(len(names) * chip_two, half)),
        16,
    )(*common, x_c, y_c, d_c, c_da, x_ab, y_ab, plane_c)
    mine = call(functools.partial(finish_second, names, chip_two, 0), partial, 10)(*common, late_weights)
    strategy, values = call(
        last_kernel, (shape(legal_mask.shape[1], par_count, jnp.float32), shape(1, par_count // 4, jnp.float32)), 4
    )(branch_counts[None, :], ancestor[None, :], legal_mask.T, b_head[None, :], mine, swap_core(theirs))
    return (strategy.T, values.reshape(-1))


def network(inputs, w_first, b_first, w_second, b_second, w_head, b_head):
    columns = inputs
    first = jnp.dot(
        columns,
        lax.all_gather(w_first, ("trav", "bulk"), axis=0, tiled=True),
        preferred_element_type=jnp.float32,
    )
    hidden_one = jnp.maximum(first + b_first, 0.0).astype(jnp.bfloat16)
    columns = hidden_one
    second = jnp.dot(
        columns,
        lax.all_gather(w_second, ("trav", "bulk"), axis=0, tiled=True),
        preferred_element_type=jnp.float32,
    )
    hidden_two = jnp.maximum(second + b_second, 0.0).astype(jnp.bfloat16)
    return jnp.dot(hidden_two, w_head, preferred_element_type=jnp.float32) + b_head


def general_body(
    parents,
    act_table,
    bucket_table,
    w_first,
    b_first,
    w_second,
    b_second,
    w_head,
    b_head,
    branch_counts,
    sampled_actions,
    bucket_owner,
    bucket_row,
    legal_mask,
    ancestor,
):
    par_count = parents.shape[0]
    feature_count = parents.shape[1]
    branch_slots = sampled_actions.shape[1]
    vocab_size = act_table.shape[0]
    action_count = w_head.shape[1]
    bulk_count = lax.axis_size("bulk")
    capacity = max(2, (4 * par_count + 3 * bulk_count - 1) // (3 * bulk_count))
    slot_total = bulk_count * capacity
    action_onehot = (
        sampled_actions.reshape(-1)[:, None] == jnp.arange(vocab_size)[None, :]
    ).astype(jnp.bfloat16)
    act_rows = jnp.dot(action_onehot, act_table, preferred_element_type=jnp.float32)
    base = (jnp.repeat(parents.astype(jnp.float32), branch_slots, axis=0) + act_rows).astype(
        jnp.bfloat16
    )
    base = lax.optimization_barrier(base)
    owner_index = bucket_owner[:, 0]
    owner_hits = (owner_index[:, None] == jnp.arange(bulk_count)[None, :]).astype(jnp.int32)
    earlier = jnp.cumsum(owner_hits, axis=0) - owner_hits
    slot_index = owner_index * capacity + jnp.sum(earlier * owner_hits, axis=1)
    placement_int = (slot_index[None, :] == jnp.arange(slot_total)[:, None]).astype(jnp.int32)
    slot_bucket = jnp.sum(placement_int * bucket_row[None, :], axis=1).reshape(bulk_count, capacity)
    placement = placement_int.astype(jnp.bfloat16)
    outgoing = jnp.dot(
        placement,
        base.reshape(par_count, branch_slots * feature_count),
        preferred_element_type=jnp.float32,
    )
    outgoing = outgoing.astype(jnp.bfloat16).reshape(
        bulk_count, capacity * branch_slots, feature_count
    )
    arrived_rows = lax.all_to_all(outgoing, "bulk", split_axis=0, concat_axis=0, tiled=True)
    arrived_ids = lax.all_to_all(slot_bucket, "bulk", split_axis=0, concat_axis=0, tiled=True)
    table_rows = jnp.take(bucket_table, arrived_ids.reshape(-1), axis=0)
    inputs = (
        arrived_rows.reshape(slot_total, branch_slots, feature_count).astype(jnp.float32)
        + table_rows.astype(jnp.float32)[:, None, :]
    )
    inputs = inputs.astype(jnp.bfloat16).reshape(slot_total * branch_slots, feature_count)
    evaluated = network(inputs, w_first, b_first, w_second, b_second, w_head, b_head)
    returned = lax.all_to_all(
        evaluated.reshape(bulk_count, capacity * branch_slots * action_count).astype(jnp.bfloat16),
        "bulk",
        split_axis=0,
        concat_axis=0,
        tiled=True,
    ).astype(jnp.float32)
    advantage = jnp.take(
        returned.reshape(slot_total, branch_slots * action_count), slot_index, axis=0
    )
    advantage = advantage.reshape(par_count, branch_slots, action_count)
    first_action = (jnp.arange(action_count) == 0).astype(jnp.float32)
    allowed = jnp.maximum(
        legal_mask.reshape(par_count, branch_slots, action_count).astype(jnp.float32), first_action
    )
    positive = allowed * (jnp.maximum(advantage, 0.0) + TREMBLE)
    sigma = positive / jnp.sum(positive, axis=-1, keepdims=True)
    live = (jnp.arange(branch_slots)[None, :] < branch_counts[:, None]).astype(jnp.float32)
    strategy = (sigma * live[:, :, None]).reshape(par_count, branch_slots * action_count)
    branch_value = jnp.sum(sigma * advantage, axis=-1)
    history_value = jnp.sum(branch_value * live, axis=1) / branch_counts.astype(jnp.float32)
    node_count = par_count // 4
    node_onehot = (ancestor[:, None] == jnp.arange(node_count)[None, :]).astype(jnp.float32)
    ancestor_value = jnp.sum(node_onehot * history_value[:, None], axis=0)
    return (strategy, ancestor_value)


def solution(mesh):
    laid_out = (mesh.shape["trav"], mesh.shape["bulk"]) == (TRAV, BULK)
    return jax.shard_map(
        body if laid_out else general_body,
        mesh=mesh,
        in_specs=(
            P(AXES, None),
            P(),
            P("bulk", None),
            P(AXES, None),
            P(),
            P(AXES, None),
            P(),
            P(),
            P(),
            P(AXES),
            P(AXES, None),
            P(AXES, None),
            P(AXES),
            P(AXES, None),
            P(AXES),
        ),
        out_specs=(P(AXES, None), P(AXES)),
        check_vma=False,
    )
```

```python
import functools

import jax
import jax.numpy as jnp
from jax import lax
from jax.experimental import pallas as pl
from jax.experimental.pallas import tpu as pltpu
from jax.sharding import PartitionSpec as P

TREMBLE = 0.05
AXES = ("trav", "bulk")

TRAV, BULK = 4, 8
X, Y, D, A, B, C = 1, 2, 3, 4, 12, 8
PLANE = (0, X, Y, D)
ID_ROWS = 16


def swap_chip(value, chip):
    return lax.ppermute(value, AXES, [(i, i ^ (chip << 1)) for i in range(TRAV * BULK)])


def swap_core(value):
    return lax.ppermute(value, AXES, [(i, i ^ 1) for i in range(TRAV * BULK)])


def iota(shape, dim):
    return lax.broadcasted_iota(jnp.int32, shape, dim)


def over_rows(a, b):
    return lax.dot_general(a, b, (((0,), (0,)), ((), ())), preferred_element_type=jnp.float32)


def my_core():
    return lax.axis_index("bulk") & 1


def my_chip():
    return lax.axis_index("trav") * (BULK // 2) + (lax.axis_index("bulk") >> 1)


def call(kernel, outs, mebibytes, scratch=()):
    many = isinstance(outs, (list, tuple))
    spec = pl.BlockSpec(memory_space=pltpu.VMEM)

    def run(*args):
        return pl.pallas_call(
            kernel,
            out_shape=tuple(outs) if many else outs,
            in_specs=[spec] * len(args),
            out_specs=(spec,) * len(outs) if many else spec,
            scratch_shapes=list(scratch),
            compiler_params=pltpu.CompilerParams(vmem_limit_bytes=mebibytes << 20),
        )(*args)

    return run


def shape(rows, columns, dtype=jnp.bfloat16):
    return jax.ShapeDtypeStruct((rows, columns), dtype)


def across(a, b, precision=None):
    return lax.dot_general(
        a, b, (((1,), (1,)), ((), ())), preferred_element_type=jnp.float32, precision=precision
    )


def keep_kernel(w_first, w_second, keep):
    one, half = w_first.shape[0], keep.shape[1]
    here = pl.ds(pl.multiple_of(my_core() * half, half), half)
    keep[:one, :] = w_first[:, here]
    keep[one:, :] = w_second[:, here]


def join_kernel(depths, keep, ids, other_first, other_second, other_owner, other_row, out, out_ids):
    core, half = my_core(), out.shape[1]
    here = pl.ds(pl.multiple_of(core * half, half), half)
    begin = 0
    for depth, other in zip(depths, (other_first, other_second)):
        for to, rows in ((core, keep[begin : begin + depth, :]), (1 - core, other[:, here])):
            place = pl.ds(pl.multiple_of(2 * begin + to * depth, depth), depth)
            for target in (out, out_ids):
                target[place, :] = rows
        begin += depth
    parts = [ref[...].astype(jnp.float32) for ref in (ids, other_owner, other_row)]
    count = ids.shape[1]
    parts = jnp.concatenate(parts + [jnp.zeros((ID_ROWS - 4, count), jnp.float32)], axis=0)
    parts = jnp.concatenate([parts, jnp.zeros((ID_ROWS, half - count), jnp.float32)], axis=1)
    out_ids[2 * begin :, :] = parts.astype(jnp.bfloat16)


def ranks_of(hits):
    count = hits.shape[1]
    before = (iota((count, count), 0) < iota((count, count), 1)).astype(jnp.bfloat16)
    return jnp.dot(hits.astype(jnp.bfloat16), before, preferred_element_type=jnp.float32)


def meta_kernel(capacity, owner, actions, out):
    partner = owner[...] ^ lax.axis_index("bulk")
    count = owner.shape[1]
    hits = (partner == iota((BULK, count), 0)).astype(jnp.float32)
    rank = jnp.sum(ranks_of(hits) * hits, axis=0, keepdims=True)
    slot = partner.astype(jnp.float32) * capacity + rank
    rows = out.shape[0]
    parts = [actions[...].astype(jnp.float32), slot, jnp.zeros((rows - actions.shape[0] - 1, count), jnp.float32)]
    parts = jnp.concatenate(parts, axis=0)
    out[...] = jnp.concatenate([parts, jnp.zeros((rows, out.shape[1] - count), jnp.float32)], axis=1).astype(jnp.bfloat16)


def serve_kernel(capacity, count, *refs):
    asked, table, outs = refs[: len(PLANE)], refs[len(PLANE)], refs[len(PLANE) + 1 :]
    buckets = table.shape[0]
    me = lax.axis_index("bulk")
    owners, rows = [], []
    for ids in asked:
        block = ids[ids.shape[0] - ID_ROWS :, :count].astype(jnp.float32)
        for core in (0, 1):
            owners.append(block[2 * core : 2 * core + 1, :])
            rows.append(block[2 * core + 1 : 2 * core + 2, :])
    owners, rows = jnp.concatenate(owners, axis=0), jnp.concatenate(rows, axis=0)
    hits = (owners.astype(jnp.int32) == me).astype(jnp.float32)
    ranks = ranks_of(hits).astype(jnp.int32)
    rows = (rows * hits).astype(jnp.bfloat16)
    wants = []
    for j in range(2 * len(PLANE)):
        at_rank = (ranks[j : j + 1, :] == iota((capacity, count), 0)).astype(jnp.bfloat16)
        wants.append(across(rows, at_rank)[j : j + 1, :])
    want = jnp.concatenate(wants, axis=1).astype(jnp.int32)
    onehot = (iota((buckets, want.shape[1]), 0) == want).astype(jnp.bfloat16)
    found = over_rows(onehot, table[...]).astype(jnp.bfloat16)
    for n, out in enumerate(outs):
        out[...] = found[2 * n * capacity : 2 * (n + 1) * capacity, :]


def inputs_kernel(capacity, branch_slots, act_table, mine, theirs, out):
    served = len(PLANE) * 2 * capacity
    rows = out.shape[0] // (2 * branch_slots)
    to = 0
    for which, ref in enumerate((mine, theirs)):
        parts = []
        for n in range(len(PLANE)):
            for core in (0, 1):
                begin = (2 * n + core) * capacity
                parts.append((mine, theirs)[which ^ core][begin : begin + capacity, :])
        buckets = jnp.concatenate(parts, axis=0)
        meta = ref[served + rows :, :rows].astype(jnp.float32).astype(jnp.int32)
        onehot = (meta[branch_slots : branch_slots + 1, :] == iota((served, rows), 0)).astype(jnp.bfloat16)
        bucket = over_rows(onehot, buckets)
        parent = ref[served : served + rows, :].astype(jnp.float32)
        acts = jnp.concatenate([meta[c : c + 1, :] for c in range(branch_slots)], axis=1)
        onehot = (acts == iota((act_table.shape[0], branch_slots * rows), 0)).astype(jnp.bfloat16)
        change = over_rows(onehot, act_table[...])
        for c in range(branch_slots):
            base = (parent + change[c * rows : (c + 1) * rows, :]).astype(jnp.bfloat16)
            out[to : to + rows, :] = (base.astype(jnp.float32) + bucket).astype(jnp.bfloat16)
            to += rows


def place_kernel(pieces, depth, *refs):
    refs, out = refs[:-1], refs[-1]
    for chip, which, begin, row, count in pieces:
        to = pl.multiple_of((my_chip() ^ chip) * depth + row, 16)
        out[pl.ds(to, count), :] = refs[which][begin : begin + count, :]


def first_kernel(depth, capacity, branch_slots, act_table, mine, theirs, home, other, bias, out, inputs):
    inputs_kernel(capacity, branch_slots, act_table, mine, theirs, inputs)
    half = home.shape[1]
    chips = half // depth
    me, core = my_chip(), my_core()
    rows, group = inputs.shape[0] // 2, 4
    for which, weights in enumerate((home, other)):
        side = core ^ which
        base = ((me // chips) ^ side) * half
        for first in range(0, chips, group):
            spots = [(n ^ me) & (chips - 1) for n in range(first, first + group)]
            columns = [pl.ds(pl.multiple_of(spot * depth, depth), depth) for spot in spots]
            shifts = [pl.ds(pl.multiple_of(side * half + spot * depth, depth), depth) for spot in spots]
            block = jnp.concatenate([weights[:, column] for column in columns], axis=1)
            shift = jnp.concatenate([bias[:, column] for column in shifts], axis=1)
            to = pl.ds(pl.multiple_of(base + first * depth, group * depth), group * depth)
            for m in (0, rows):
                total = jnp.dot(inputs[m : m + rows, :], block, preferred_element_type=jnp.float32)
                out[m : m + rows, to] = jnp.maximum(total + shift, 0.0).astype(jnp.bfloat16)


def line_up(pieces, refs, depth, weights):
    order = list(dict.fromkeys(piece[0] for piece in pieces))
    for name, which, begin, row, count in pieces:
        to = order.index(name) * depth + row
        weights[to : to + count, :] = refs[which][begin : begin + count, :]
    return [slice(name * depth, (name + 1) * depth) for name in order]


def second_kernel(pieces, depth, hidden, *refs):
    refs, (out, weights) = refs[:-2], refs[-2:]
    columns = line_up(pieces, refs, depth, weights)
    step, rows = 512, hidden.shape[0] // 2
    for m in (0, rows):
        picked = jnp.concatenate([hidden[m : m + rows, column] for column in columns], axis=1)
        for n in range(0, out.shape[1], step):
            out[m : m + rows, n : n + step] = jnp.dot(
                picked, weights[:, n : n + step], preferred_element_type=jnp.float32
            )


def finish_second(names, depth, first, hidden, so_far, bias, w_head, weights, out):
    half, core, rows = so_far.shape[1], my_core(), out.shape[1]
    here = slice(first, first + rows)
    picked = jnp.concatenate([hidden[here, name * depth : (name + 1) * depth] for name in names], axis=1)
    advantage = jnp.zeros((rows, w_head.shape[0]), jnp.float32)
    step = 512
    for n in range(0, half, step):
        columns = pl.ds(pl.multiple_of(core * half + n, step), step)
        total = so_far[here, n : n + step] + jnp.dot(
            picked, weights[:, n : n + step], preferred_element_type=jnp.float32
        )
        layer = jnp.maximum(total + bias[:, columns], 0.0).astype(jnp.bfloat16)
        advantage = advantage + across(layer, w_head[:, columns])
    out[...] = advantage.T


def theirs_kernel(pieces, names, depth, first, hidden, so_far, bias, w_head, *refs):
    refs, (out, weights) = refs[:-2], refs[-2:]
    line_up(pieces, refs, depth, weights)
    finish_second(names, depth, first, hidden, so_far, bias, w_head, weights, out)


def stack_kernel(places, *refs):
    refs, out = refs[:-1], refs[-1]
    to = 0
    for ref, (begin, count) in zip(refs, places):
        out[to : to + count, :] = ref[begin : begin + count, :]
        to += count


def stack(*parts):
    arrays, places = [part[0] for part in parts], [part[1:] for part in parts]
    total = sum(count for _, count in places)
    out = shape(total, arrays[0].shape[1], arrays[0].dtype)
    return call(functools.partial(stack_kernel, places), out, 4)(*arrays)


def last_kernel(counts, ancestor, legal, b_head, mine, theirs, strategy, values):
    actions = b_head.shape[1]
    rows = counts.shape[1]
    diagonal = iota((actions, actions), 0) == iota((actions, actions), 1)
    shift = jnp.sum(jnp.where(diagonal, b_head[...], 0.0), axis=1, keepdims=True)
    first_action = (iota((actions, rows), 0) == 0).astype(jnp.float32)
    total_value = jnp.zeros((1, rows), jnp.float32)
    for c in range(mine.shape[1] // rows):
        here = slice(c * rows, (c + 1) * rows)
        advantage = mine[:, here] + theirs[:, here] + shift
        allowed = jnp.maximum(legal[c * actions : (c + 1) * actions, :].astype(jnp.float32), first_action)
        positive = allowed * (jnp.maximum(advantage, 0.0) + TREMBLE)
        sigma = positive / jnp.sum(positive, axis=0, keepdims=True)
        live = (counts[...] > c).astype(jnp.float32)
        strategy[c * actions : (c + 1) * actions, :] = sigma * live
        total_value = total_value + live * jnp.sum(sigma * advantage, axis=0, keepdims=True)
    value = total_value / counts[...].astype(jnp.float32)
    at_node = (ancestor[...] == iota((values.shape[1], rows), 0)).astype(jnp.float32)
    values[...] = across(value, at_node, lax.Precision.HIGHEST)


def body(
    parents,
    act_table,
    bucket_table,
    w_first,
    b_first,
    w_second,
    b_second,
    w_head,
    b_head,
    branch_counts,
    sampled_actions,
    bucket_owner,
    bucket_row,
    legal_mask,
    ancestor,
):
    par_count, feature_count = parents.shape
    branch_slots = sampled_actions.shape[1]
    branches = par_count * branch_slots
    hidden_units = w_first.shape[1]
    half = hidden_units // 2
    depth_one, depth_two = w_first.shape[0], w_second.shape[0]
    chip_one, chip_two = 2 * depth_one, 2 * depth_two
    depth = chip_one + chip_two
    capacity = max(2, (4 * par_count + 3 * BULK - 1) // (3 * BULK))
    wide = 2 * capacity

    owner, row = bucket_owner.T, bucket_row[None, :]
    keep = call(keep_kernel, shape(depth // 2, half), 4)(w_first, w_second)
    ids = jnp.concatenate([owner, row], axis=0)
    own, own_ids = call(
        functools.partial(join_kernel, (depth_one, depth_two)), (shape(depth, half), shape(depth + ID_ROWS, half)), 4
    )(keep, ids, swap_core(w_first), swap_core(w_second), swap_core(owner), swap_core(row))
    from_x, from_y, from_d = [swap_chip(own_ids, chip) for chip in PLANE[1:]]
    from_a, from_b = [swap_chip(own, chip) for chip in (A, B)]
    meta = call(functools.partial(meta_kernel, capacity), shape(ID_ROWS, feature_count), 4)(owner, sampled_actions.T)
    table = stack((bucket_table, 0, bucket_table.shape[0]))
    from_x, from_y, from_d, from_a, table = lax.optimization_barrier((from_x, from_y, from_d, from_a, table))

    served = call(
        functools.partial(serve_kernel, capacity, par_count), (shape(wide, feature_count),) * len(PLANE), 6
    )(own_ids, from_x, from_y, from_d, table)
    some = chip_one // 4
    few, rest = chip_one // 4, 3 * chip_two // 8
    x_ab = swap_chip(
        stack(
            (from_a, few, depth - few), (from_b, 0, chip_one), (from_b, chip_one + rest, chip_two - rest),
            (served[1], 0, wide)
        ),
        X,
    )
    y_ab = swap_chip(stack((from_a, few, depth - few), (from_b, 0, depth - rest), (served[2], 0, wide)), Y)
    rows_d = swap_chip(stack((served[3], 0, wide), (from_b, 0, chip_one)), D)
    c_da = swap_chip(stack((from_b, 0, depth), (from_d, 0, chip_one), (from_x, 0, few), (from_y, 0, few)), A)
    plane_c = swap_chip(stack((from_x, 0, chip_one), (from_y, 0, chip_one), (from_d, 0, chip_one + some)), C)
    x_ab, y_ab, rows_d, c_da, plane_c = lax.optimization_barrier((x_ab, y_ab, rows_d, c_da, plane_c))

    cut = chip_two // 2
    at_a, at_b = chip_one - few, depth - few + chip_one
    x_c = swap_chip(
        stack((c_da, chip_one, chip_two), (y_ab, at_a, cut), (y_ab, at_b, cut), (from_b, chip_one, rest)), X
    )
    y_c = swap_chip(
        stack(
            (c_da, chip_one, chip_two), (x_ab, at_a + cut, cut), (x_ab, at_b + cut - rest, cut),
            (from_b, depth - rest, rest)
        ),
        Y,
    )
    d_c = swap_chip(stack((from_d, chip_one + some, chip_two - some)), C)

    end = 2 * depth - few - rest
    mine_rows = stack(
        (served[0], 0, wide), (x_ab, end, wide), (y_ab, end, wide), (rows_d, 0, wide),
        (parents, 0, par_count), (meta, 0, ID_ROWS)
    )
    arrays = [own, from_x, from_y, from_a, from_b, from_d, x_ab, y_ab, c_da]
    near = [(chip, n) for n, chip in enumerate((0, X, Y, A, B, D))]
    first_pieces = [(chip, n, 0, 0, chip_one) for chip, n in near] + [(C, 8, 0, 0, chip_one)]
    for n, chip in ((6, X), (7, Y)):
        first_pieces.append((chip ^ A, 8, depth + chip_one + (n - 6) * few, 0, few))
        first_pieces += [(chip ^ A, n, 0, few, chip_one - few), (chip ^ B, n, depth - few, 0, chip_one)]
    first_pieces += [(D ^ A, 8, depth, 0, chip_one), (D ^ B, 9, wide, 0, chip_one)]
    first_pieces += [(chip ^ C, 10, n * chip_one, 0, chip_one) for n, chip in enumerate((X, Y, D))]
    weights = call(functools.partial(place_kernel, first_pieces, chip_one), shape(feature_count, half), 4)(
        *arrays, rows_d, plane_c
    )
    hidden = call(
        functools.partial(first_kernel, chip_two, capacity, branch_slots),
        shape(2 * branches, hidden_units),
        16,
        [pltpu.VMEM((2 * branches, feature_count), jnp.bfloat16)],
    )(act_table, mine_rows, swap_core(mine_rows), weights, swap_core(weights), b_first[None, :])

    early = [(chip, n, chip_one, 0, chip_two) for chip, n in near]
    for n, chip in ((6, X), (7, Y)):
        early.append((chip ^ A, n, at_a, 0, chip_two))
    early.sort()
    so_far = call(
        functools.partial(second_kernel, early, chip_two),
        shape(2 * branches, half, jnp.float32),
        16,
        [pltpu.VMEM((len({piece[0] for piece in early}) * chip_two, half), jnp.bfloat16)],
    )(hidden, *arrays)
    late = [(C, 3, chip_one, 0, chip_two), (X ^ C, 0, 0, 0, chip_two), (Y ^ C, 1, 0, 0, chip_two)]
    late += [(D ^ C, 6, 3 * chip_one, 0, some), (D ^ C, 2, 0, some, chip_two - some)]
    late += [(D ^ A, 0, chip_two, 0, cut), (D ^ A, 1, chip_two, cut, cut)]
    late += [(D ^ B, 0, chip_two + cut, 0, cut), (D ^ B, 1, chip_two + cut, cut, cut)]
    tail = chip_two + 2 * cut
    late += [(X ^ B, 4, at_b, rest, chip_two - rest), (X ^ B, 0, tail, 0, rest)]
    late += [(Y ^ B, 5, at_b, 0, chip_two - rest), (Y ^ B, 1, tail, chip_two - rest, rest)]
    names = list(dict.fromkeys(piece[0] for piece in late))
    partial = shape(w_head.shape[1], branches, jnp.float32)
    common = (hidden, so_far, b_second[None, :], w_head.T)
    theirs, late_weights = call(
        functools.partial(theirs_kernel, late, names, chip_two, branches),
        (partial, shape(len(names) * chip_two, half)),
        16,
    )(*common, x_c, y_c, d_c, c_da, x_ab, y_ab, plane_c)
    mine = call(functools.partial(finish_second, names, chip_two, 0), partial, 10)(*common, late_weights)
    strategy, values = call(
        last_kernel, (shape(legal_mask.shape[1], par_count, jnp.float32), shape(1, par_count // 4, jnp.float32)), 4
    )(branch_counts[None, :], ancestor[None, :], legal_mask.T, b_head[None, :], mine, swap_core(theirs))
    return (strategy.T, values.reshape(-1))


def network(inputs, w_first, b_first, w_second, b_second, w_head, b_head):
    columns = inputs
    first = jnp.dot(
        columns,
        lax.all_gather(w_first, ("trav", "bulk"), axis=0, tiled=True),
        preferred_element_type=jnp.float32,
    )
    hidden_one = jnp.maximum(first + b_first, 0.0).astype(jnp.bfloat16)
    columns = hidden_one
    second = jnp.dot(
        columns,
        lax.all_gather(w_second, ("trav", "bulk"), axis=0, tiled=True),
        preferred_element_type=jnp.float32,
    )
    hidden_two = jnp.maximum(second + b_second, 0.0).astype(jnp.bfloat16)
    return jnp.dot(hidden_two, w_head, preferred_element_type=jnp.float32) + b_head


def general_body(
    parents,
    act_table,
    bucket_table,
    w_first,
    b_first,
    w_second,
    b_second,
    w_head,
    b_head,
    branch_counts,
    sampled_actions,
    bucket_owner,
    bucket_row,
    legal_mask,
    ancestor,
):
    par_count = parents.shape[0]
    feature_count = parents.shape[1]
    branch_slots = sampled_actions.shape[1]
    vocab_size = act_table.shape[0]
    action_count = w_head.shape[1]
    bulk_count = lax.axis_size("bulk")
    capacity = max(2, (4 * par_count + 3 * bulk_count - 1) // (3 * bulk_count))
    slot_total = bulk_count * capacity
    action_onehot = (
        sampled_actions.reshape(-1)[:, None] == jnp.arange(vocab_size)[None, :]
    ).astype(jnp.bfloat16)
    act_rows = jnp.dot(action_onehot, act_table, preferred_element_type=jnp.float32)
    base = (jnp.repeat(parents.astype(jnp.float32), branch_slots, axis=0) + act_rows).astype(
        jnp.bfloat16
    )
    base = lax.optimization_barrier(base)
    owner_index = bucket_owner[:, 0]
    owner_hits = (owner_index[:, None] == jnp.arange(bulk_count)[None, :]).astype(jnp.int32)
    earlier = jnp.cumsum(owner_hits, axis=0) - owner_hits
    slot_index = owner_index * capacity + jnp.sum(earlier * owner_hits, axis=1)
    placement_int = (slot_index[None, :] == jnp.arange(slot_total)[:, None]).astype(jnp.int32)
    slot_bucket = jnp.sum(placement_int * bucket_row[None, :], axis=1).reshape(bulk_count, capacity)
    placement = placement_int.astype(jnp.bfloat16)
    outgoing = jnp.dot(
        placement,
        base.reshape(par_count, branch_slots * feature_count),
        preferred_element_type=jnp.float32,
    )
    outgoing = outgoing.astype(jnp.bfloat16).reshape(
        bulk_count, capacity * branch_slots, feature_count
    )
    arrived_rows = lax.all_to_all(outgoing, "bulk", split_axis=0, concat_axis=0, tiled=True)
    arrived_ids = lax.all_to_all(slot_bucket, "bulk", split_axis=0, concat_axis=0, tiled=True)
    table_rows = jnp.take(bucket_table, arrived_ids.reshape(-1), axis=0)
    inputs = (
        arrived_rows.reshape(slot_total, branch_slots, feature_count).astype(jnp.float32)
        + table_rows.astype(jnp.float32)[:, None, :]
    )
    inputs = inputs.astype(jnp.bfloat16).reshape(slot_total * branch_slots, feature_count)
    evaluated = network(inputs, w_first, b_first, w_second, b_second, w_head, b_head)
    returned = lax.all_to_all(
        evaluated.reshape(bulk_count, capacity * branch_slots * action_count).astype(jnp.bfloat16),
        "bulk",
        split_axis=0,
        concat_axis=0,
        tiled=True,
    ).astype(jnp.float32)
    advantage = jnp.take(
        returned.reshape(slot_total, branch_slots * action_count), slot_index, axis=0
    )
    advantage = advantage.reshape(par_count, branch_slots, action_count)
    first_action = (jnp.arange(action_count) == 0).astype(jnp.float32)
    allowed = jnp.maximum(
        legal_mask.reshape(par_count, branch_slots, action_count).astype(jnp.float32), first_action
    )
    positive = allowed * (jnp.maximum(advantage, 0.0) + TREMBLE)
    sigma = positive / jnp.sum(positive, axis=-1, keepdims=True)
    live = (jnp.arange(branch_slots)[None, :] < branch_counts[:, None]).astype(jnp.float32)
    strategy = (sigma * live[:, :, None]).reshape(par_count, branch_slots * action_count)
    branch_value = jnp.sum(sigma * advantage, axis=-1)
    history_value = jnp.sum(branch_value * live, axis=1) / branch_counts.astype(jnp.float32)
    node_count = par_count // 4
    node_onehot = (ancestor[:, None] == jnp.arange(node_count)[None, :]).astype(jnp.float32)
    ancestor_value = jnp.sum(node_onehot * history_value[:, None], axis=0)
    return (strategy, ancestor_value)


def solution(mesh):
    laid_out = (mesh.shape["trav"], mesh.shape["bulk"]) == (TRAV, BULK)
    return jax.shard_map(
        body if laid_out else general_body,
        mesh=mesh,
        in_specs=(
            P(AXES, None),
            P(),
            P("bulk", None),
            P(AXES, None),
            P(),
            P(AXES, None),
            P(),
            P(),
            P(),
            P(AXES),
            P(AXES, None),
            P(AXES, None),
            P(AXES),
            P(AXES, None),
            P(AXES),
        ),
        out_specs=(P(AXES, None), P(AXES)),
        check_vma=False,
    )
```
